32 devices in a mesh: slab: 2 (over x), tile: 16 (over z, y, core).
Axes of the slice: x: 2, y: 2, z: 4, core: 2. Of those that a mesh axis runs over, the one named last changes fastest.
Arguments:
- estimate: float32 [256, 32, 128], P(('slab', 'tile')), parts along dimension 0, may hold values from 0.5 to 2
- observed: bfloat16 [8, 256, 32, 128], P(None, ('slab', 'tile')), parts along dimension 1, may hold values from 0.5 to 2
- interp: bfloat16 [8, 256, 32, 128], P(None, ('slab', 'tile')), parts along dimension 1, may hold values from 0 to 1
- source_rows: int32 [8, 256, 32], P(None, ('slab', 'tile')), parts along dimension 1, may hold values from 0 to 127, as said below
- tissue: int32 [256], P(('slab', 'tile')), parts along dimension 0, may hold values 0 or 1
- psf_x: float32 [8, 9], replicated, may hold values from 0.1 to 1
- psf_y: float32 [8, 9], replicated, may hold values from 0.1 to 1
- psf_z: float32 [8, 33], replicated, may hold values from 0.05 to 1
Outputs:
- refined: float32 [256, 32, 128], P(('slab', 'tile')), parts along dimension 0
The draws below stay inside these ranges and needn't reach their ends.
There are 2 independent parts, one for each index of `slab`. The reference program is written for one: setup_inputs(seed, part) draws one part's arguments, and reference() takes and returns one part's arrays. A program takes and returns all parts, laid end to end along the dimension named above; an argument that names none is the same for every part. Nothing has to cross between parts.
Inputs may be any that keep to these rules, and one draw needn't show every extreme that they name: `source_rows`: for each view, among the 8 x 32 joining lines of one device at most 32 take their source row from the rows of any one device, and some device's lines reach 32 from one device.
All inputs are finite; a program needn't handle non-finite values. No bound on the sum of `tissue` on one device may be relied on, other than what follows from the above.
Results may differ from the reference program's by a relative error of at most 0.0014.
Values may be sent and summed in bfloat16 or wider, within the bound.
A program may use at most 64 MiB of HBM per device.

```python
import math
import jax
import jax.numpy as jnp
from jax import lax

V = 8
TX = 8
Z = 32
Y = 128
KXY = 9
KZ = 33
NX = 128
N_TILE = 16


def draw_source_rows(key, part):
    key = jax.random.fold_in(key, 11)
    line_count = TX * Z
    capacity = 2 * line_count // N_TILE
    pair_count = N_TILE // 2

    def one_block(block_key):
        key_split, key_owner, key_row, key_order = jax.random.split(block_key, 4)
        splits = jax.random.randint(key_split, (pair_count,), 0, capacity + 1)
        splits = splits.at[0].set(capacity)
        position = jnp.arange(line_count)
        pair_index = position // capacity
        within = position - pair_index * capacity
        owner_slot = 2 * pair_index + (within >= splits[pair_index]).astype(jnp.int32)
        owner = jax.random.permutation(key_owner, N_TILE)[owner_slot]
        row_pick = jax.random.randint(key_row, (line_count,), 0, TX)
        source = owner * TX + row_pick
        order = jax.random.permutation(key_order, line_count)
        return source[order]
    block_keys = jax.random.split(key, V * N_TILE)
    drawn = jax.vmap(one_block)(block_keys)
    return drawn.reshape(V, N_TILE * TX, Z).astype(jnp.int32)


def set_ends(array, stream_key, smallest, top_value):
    longest = array.shape.index(max(array.shape))
    spots = []
    for shift in (0, 1):
        where = [jax.random.randint(jax.random.fold_in(stream_key, axis), (), 0, length) for axis, length in enumerate(array.shape)]
        where[longest] = (where[longest] + shift) % array.shape[longest]
        spots.append(tuple(where))
    return array.at[spots[0]].set(smallest).at[spots[1]].set(top_value)


def shard_levels(rng, shape, pieces, smallest, largest):
    gain, own = 1.0, jax.random.fold_in(rng, 6)
    for dim, parts in pieces:
        draws = jnp.exp(jax.random.uniform(jax.random.fold_in(own, dim), (parts,), jnp.float32, smallest / len(pieces), largest / len(pieces)))
        gain = gain * jnp.repeat(draws, shape[dim] // parts).reshape([-1 if axis == dim else 1 for axis in range(len(shape))])
    return gain


def setup_inputs(seed: int = 0, part: int = 0) -> dict:
    streams_of = jax.random.split(jax.random.key(seed), 9)
    own_keys = jax.random.split(jax.random.fold_in(streams_of[8], part), 9)
    estimate = jnp.clip(jnp.exp(math.log(2.0) - 1.3862944 * jax.random.uniform(own_keys[0], (NX, Z, Y), jnp.float32) ** shard_levels(own_keys[0], (NX, Z, Y), ((0, 16),), -0.2, 0.2)), 0.5, 2.0)
    observed = jnp.clip(jnp.exp(math.log(2.0) - 1.3862944 * jax.random.uniform(own_keys[1], (V, NX, Z, Y), jnp.float32) ** shard_levels(own_keys[1], (V, NX, Z, Y), ((1, 16),), -0.2, 0.2)), 0.5, 2.0).astype(jnp.bfloat16)
    interp = jnp.clip(1.0 * jax.random.uniform(own_keys[2], (V, NX, Z, Y), jnp.float32) ** shard_levels(own_keys[2], (V, NX, Z, Y), ((1, 16),), -0.2, 0.2), 0.0, 1.0).astype(jnp.bfloat16)
    source_rows = draw_source_rows(jax.random.fold_in(jax.random.fold_in(streams_of[8], part), 71), part)
    tissue = set_ends((jax.random.randint(own_keys[4], (NX,), 0, 4) < 3).astype(jnp.int32), jax.random.fold_in(own_keys[4], 1), 0, 1)
    psf_x = jnp.clip(jnp.exp(jax.random.uniform(streams_of[5], (V, KXY), jnp.float32, math.log(0.1), math.log(1.0))), 0.1, 1.0)
    psf_y = jnp.clip(jnp.exp(jax.random.uniform(streams_of[6], (V, KXY), jnp.float32, math.log(0.1), math.log(1.0))), 0.1, 1.0)
    psf_z = jnp.clip(jnp.exp(jax.random.uniform(streams_of[7], (V, KZ), jnp.float32, math.log(0.05), math.log(1.0))), 0.05, 1.0)
    return {"estimate": estimate, "observed": observed, "interp": interp, "source_rows": source_rows, "tissue": tissue, "psf_x": psf_x, "psf_y": psf_y, "psf_z": psf_z}


def taps_matrix(coeffs, count):
    half_taps = coeffs.shape[0] // 2
    offsets = jnp.arange(count)[:, None] - jnp.arange(count)[None, :] + half_taps
    inside = (offsets >= 0) & (offsets < coeffs.shape[0])
    return jnp.where(inside, coeffs[jnp.clip(offsets, 0, coeffs.shape[0] - 1)], jnp.float32(0.0))


def forward_x(volume, coeffs):
    half_taps = coeffs.shape[0] // 2
    padded = jnp.pad(volume, ((half_taps, half_taps), (0, 0), (0, 0)))
    count = volume.shape[0]
    result = jnp.zeros_like(volume)
    for offset in range(coeffs.shape[0]):
        result = result + coeffs[offset] * padded[offset:offset + count]
    return result


def adjoint_x(volume, coeffs):
    half_taps = coeffs.shape[0] // 2
    padded = jnp.pad(volume, ((half_taps, half_taps), (0, 0), (0, 0)))
    count = volume.shape[0]
    result = jnp.zeros_like(volume)
    for offset in range(coeffs.shape[0]):
        start = 2 * half_taps - offset
        result = result + coeffs[offset] * padded[start:start + count]
    return result


def reference(estimate, observed, interp, source_rows, tissue, psf_x, psf_y, psf_z):
    depth_cells = estimate.shape[1]
    lane_cells = estimate.shape[2]
    view_count = observed.shape[0]
    running = jnp.zeros_like(estimate)
    planes = jnp.arange(depth_cells)[None, :]
    for view in range(view_count):
        taps_x = psf_x[view] / jnp.sum(psf_x[view])
        taps_y = psf_y[view] / jnp.sum(psf_y[view])
        taps_z = psf_z[view] / jnp.sum(psf_z[view])
        matrix_z = taps_matrix(taps_z, depth_cells)
        matrix_y = taps_matrix(taps_y, lane_cells)
        source_line = observed[view][source_rows[view], planes, :].astype(jnp.float32)
        next_line = jnp.concatenate([source_line[..., 1:], source_line[..., -1:]], axis=2)
        weight = interp[view].astype(jnp.float32)
        joined_view = weight * source_line + (1.0 - weight) * next_line
        blurred = forward_x(estimate, taps_x)
        blurred = jnp.einsum("xzy,zw->xwy", blurred, matrix_z, precision=lax.Precision.HIGHEST)
        blurred = jnp.einsum("xzy,yu->xzu", blurred, matrix_y, precision=lax.Precision.HIGHEST)
        quotient = joined_view / blurred
        corrected = jnp.einsum("xzu,yu->xzy", quotient, matrix_y, precision=lax.Precision.HIGHEST)
        corrected = jnp.einsum("xwy,zw->xzy", corrected, matrix_z, precision=lax.Precision.HIGHEST)
        running = running + adjoint_x(corrected, taps_x)
    updated = estimate * running / view_count
    return jnp.where(tissue[:, None, None] == 1, updated, estimate)
```

```python
import functools

import jax
import jax.numpy as jnp
from jax import lax
from jax.experimental import pallas as pl
from jax.experimental.pallas import tpu as pltpu
from jax.sharding import PartitionSpec as P


def extended_2(value, sides, width):
    for axis, dim in sides:
        size, length = (lax.axis_size(axis), value.shape[dim])
        up = [(i, (i + 1) % size) for i in range(size - 1)]
        down = [(j, i) for i, j in up]
        last = lax.slice_in_dim(value, length - width, length, axis=dim)
        first = lax.slice_in_dim(value, 0, width, axis=dim)
        before = lax.ppermute(last, axis, up)
        after = lax.ppermute(first, axis, down)
        value = jnp.concatenate([before, value, after], axis=dim)
    return value


def taps_matrix(coeffs, count):
    half_taps = coeffs.shape[0] // 2
    offsets = jnp.arange(count)[:, None] - jnp.arange(count)[None, :] + half_taps
    inside = (offsets >= 0) & (offsets < coeffs.shape[0])
    return jnp.where(inside, coeffs[jnp.clip(offsets, 0, coeffs.shape[0] - 1)], jnp.float32(0.0))


def forward_x(extended, coeffs, out_rows):
    result = coeffs[0] * extended[0:out_rows]
    for offset in range(1, coeffs.shape[0]):
        result = result + coeffs[offset] * extended[offset : offset + out_rows]
    return result


def adjoint_x(extended, coeffs, out_rows):
    half_taps = coeffs.shape[0] // 2
    result = jnp.zeros((out_rows,) + extended.shape[1:], jnp.float32)
    for offset in range(coeffs.shape[0]):
        start = 2 * half_taps - offset
        result = result + coeffs[offset] * extended[start : start + out_rows]
    return result


def forward_yz(volume, matrix_z, matrix_y):
    volume = jnp.einsum("xzy,zw->xwy", volume, matrix_z, precision=lax.Precision.HIGHEST)
    return jnp.einsum("xzy,yu->xzu", volume, matrix_y, precision=lax.Precision.HIGHEST)


def adjoint_yz(volume, matrix_z, matrix_y):
    volume = jnp.einsum("xzu,yu->xzy", volume, matrix_y, precision=lax.Precision.HIGHEST)
    return jnp.einsum("xwy,zw->xzy", volume, matrix_z, precision=lax.Precision.HIGHEST)


def body_by_collectives(estimate, observed, interp, source_rows, tissue, psf_x, psf_y, psf_z):
    tile_rows, depth_cells, lane_cells = estimate.shape
    view_count = observed.shape[0]
    tile_count = lax.axis_size("tile")
    line_count = tile_rows * depth_cells
    capacity = 2 * line_count // tile_count
    half_taps = psf_x.shape[1] // 2
    flat_obs = observed.reshape(view_count * line_count, lane_cells)
    owners = (source_rows // tile_rows).reshape(view_count, line_count)
    payload = (
        jnp.arange(view_count, dtype=jnp.int32)[:, None, None] * line_count
        + source_rows % tile_rows * depth_cells
        + jnp.arange(depth_cells, dtype=jnp.int32)[None, None, :]
    ).reshape(view_count, line_count)
    owner_hits = (
        owners[:, :, None] == jnp.arange(tile_count, dtype=jnp.int32)[None, None, :]
    ).astype(jnp.int32)
    slot_index = jnp.sum((jnp.cumsum(owner_hits, axis=1) - 1) * owner_hits, axis=2)
    view_column = jnp.broadcast_to(
        jnp.arange(view_count, dtype=jnp.int32)[:, None], (view_count, line_count)
    )
    requests = jnp.zeros((tile_count, view_count, capacity), jnp.int32)
    requests = requests.at[owners, view_column, slot_index].set(payload)
    returned = lax.all_to_all(
        flat_obs[lax.all_to_all(requests, "tile", split_axis=0, concat_axis=0, tiled=True)],
        "tile",
        split_axis=0,
        concat_axis=0,
        tiled=True,
    )
    gathered_lines = returned[owners, view_column, slot_index]
    extended = extended_2(estimate.astype(jnp.bfloat16), (("tile", 0),), half_taps).astype(
        estimate.dtype
    )
    running = jnp.zeros_like(estimate)
    for view in range(view_count):
        taps_x = psf_x[view] / jnp.sum(psf_x[view])
        taps_y = psf_y[view] / jnp.sum(psf_y[view])
        taps_z = psf_z[view] / jnp.sum(psf_z[view])
        matrix_z = taps_matrix(taps_z, depth_cells)
        matrix_y = taps_matrix(taps_y, lane_cells)
        view_lines = gathered_lines[view]
        source_line = view_lines.reshape(tile_rows, depth_cells, lane_cells).astype(jnp.float32)
        next_line = jnp.concatenate([source_line[..., 1:], source_line[..., -1:]], axis=2)
        weight = interp[view].astype(jnp.float32)
        joined_view = weight * source_line + (1.0 - weight) * next_line
        blurred = forward_yz(forward_x(extended, taps_x, tile_rows), matrix_z, matrix_y)
        quotient = joined_view / blurred
        corrected = adjoint_yz(quotient, matrix_z, matrix_y)
        corrected_band = extended_2(
            corrected.astype(jnp.bfloat16), (("tile", 0),), half_taps
        ).astype(corrected.dtype)
        running = running + adjoint_x(corrected_band, taps_x, tile_rows)
    updated = estimate * running / view_count
    return jnp.where(tissue[:, None, None] == 1, updated, estimate)


MESH = pl.DeviceIdType.MESH
F32 = jnp.float32
BF16 = jnp.bfloat16


def split(value):
    high = value.astype(BF16)
    return high, (value - high.astype(F32)).astype(BF16)


def dot(left, right):
    return jnp.dot(left, right, preferred_element_type=F32)


def dot_split(left, right):
    return dot(left[0], right[0]) + dot(left[0], right[1]) + dot(left[1], right[0])


def one_hot(mask):
    return jnp.where(mask, 1.0, 0.0).astype(BF16)


def sweep_kernel(
    n, est, obs, interp, rows, px, py, pz, out,
    ext, halo_out, halo_in, req_out, req_in, req_t, slot_t, unpack, send, recv,
    inverse, adj_z, adj_y, acc, sum_out, sum_in,
    halo_send_sem, halo_recv_sem, req_send_sem, req_recv_sem, line_send_sem, line_recv_sem,
    sum_send_sem, sum_recv_sem,
):
    x_rows, depth, lanes = est.shape
    views = obs.shape[0]
    lines = x_rows * depth
    cap = 2 * lines // n
    slots = n * cap
    per_block = lanes // cap
    taps = px.shape[1]
    taps_z = pz.shape[1]
    half = taps // 2
    edge = half * depth
    me = lax.axis_index("tile")

    barrier = pltpu.get_barrier_semaphore()

    @pl.loop(1, n)
    def _(j):
        pl.semaphore_signal(barrier, inc=1, device_id={"tile": lax.rem(me + j, n)}, device_id_type=MESH)

    halo_out[0] = est[0:half].reshape(edge, lanes).astype(BF16)
    halo_out[1] = est[x_rows - half : x_rows].reshape(edge, lanes).astype(BF16)

    wanted = rows[...]
    owner = wanted // x_rows
    line_id = lax.broadcasted_iota(jnp.int32, (views, lines), 1)
    payload = ((wanted - owner * x_rows) * depth + lax.rem(line_id, depth)).astype(F32)
    hits = [jnp.where(owner == o, 1.0, 0.0) for o in range(n)]
    earlier = one_hot(
        lax.broadcasted_iota(jnp.int32, (lines, lines), 0) < lax.broadcasted_iota(jnp.int32, (lines, lines), 1)
    )
    rank = dot(jnp.concatenate(hits, axis=0).astype(BF16), earlier)
    slot = jnp.zeros((views, lines), F32)
    for o in range(n):
        slot = slot + hits[o] * (rank[o * views : (o + 1) * views] + float(o * cap))
    padded = jnp.concatenate([slot, jnp.zeros((lanes - views, lines), F32)], axis=0)
    slot_t[...] = padded.T

    view_row = lax.broadcasted_iota(jnp.int32, (views, lines), 0)
    slot_lane = lax.broadcasted_iota(jnp.int32, (lines, slots), 1).astype(F32)

    def request(v, total):
        column = pltpu.roll(slot_t[...], lax.rem(lanes - v, lanes), 1)[:, 0:1]
        chosen = one_hot(column == slot_lane)
        unpack[v] = chosen
        return total + dot(jnp.where(view_row == v, payload, 0.0).astype(BF16), chosen)

    requests = lax.fori_loop(0, views, request, jnp.zeros((views, slots), F32))
    for b in range(slots // lanes):
        req_out[b] = requests[:, b * lanes : (b + 1) * lanes]

    pl.semaphore_wait(barrier, n - 1)

    def halo_copy(source, target, send_sem, recv_sem, side, device):
        return pltpu.make_async_remote_copy(
            src_ref=source.at[side], dst_ref=target.at[1 - side],
            send_sem=send_sem.at[side], recv_sem=recv_sem.at[1 - side],
            device_id={"tile": device}, device_id_type=MESH,
        )

    def to_prev(source, target, send_sem, recv_sem):
        return halo_copy(source, target, send_sem, recv_sem, 0, lax.rem(me + n - 1, n))

    def to_next(source, target, send_sem, recv_sem):
        return halo_copy(source, target, send_sem, recv_sem, 1, lax.rem(me + 1, n))

    def request_copy(j):
        d = lax.rem(me + j, n)
        return pltpu.make_async_remote_copy(
            src_ref=req_out.at[d // per_block], dst_ref=req_in.at[me],
            send_sem=req_send_sem, recv_sem=req_recv_sem,
            device_id={"tile": d}, device_id_type=MESH,
        )

    @pl.loop(1, n)
    def _(j):
        request_copy(j).start()

    halos = (halo_out, halo_in, halo_send_sem, halo_recv_sem)

    @pl.when(me > 0)
    def _():
        to_prev(*halos).start()

    @pl.when(me < n - 1)
    def _():
        to_next(*halos).start()

    req_in[me] = req_out[me // per_block]
    ahead = pl.ds(0, n - 1)
    pltpu.make_async_copy(req_in.at[ahead], req_in.at[ahead], req_recv_sem).wait()
    pltpu.make_async_copy(req_in.at[ahead], req_in.at[ahead], req_send_sem).wait()

    req_t[...] = req_in[...].reshape(n * views, lanes).T
    mine = req_t[pl.ds(lax.rem(me, per_block) * cap, cap), :]
    line_lane = lax.broadcasted_iota(jnp.int32, (cap, lines), 1).astype(F32)
    own = pl.ds(pl.multiple_of(me * cap, cap), cap)

    @pl.loop(0, views)
    def _(v):
        turned = pltpu.roll(mine, lax.rem(lanes - v, lanes), 1)
        chosen = jnp.concatenate(
            [one_hot(turned[:, d * views : d * views + 1] == line_lane) for d in range(n)], axis=0
        )
        send[v] = dot(chosen, obs[v].reshape(lines, lanes)).astype(BF16)

        @pl.loop(1, n)
        def _(j):
            d = lax.rem(me + j, n)
            pltpu.make_async_remote_copy(
                src_ref=send.at[v, pl.ds(pl.multiple_of(d * cap, cap), cap)], dst_ref=recv.at[v, own],
                send_sem=line_send_sem.at[v], recv_sem=line_recv_sem.at[v],
                device_id={"tile": d}, device_id_type=MESH,
            ).start()

        recv[v, own] = send[v, own]

    ext[half : half + x_rows] = est[...]

    @pl.when(me > 0)
    def _():
        to_prev(*halos).wait_send()
        pltpu.make_async_copy(halo_in.at[0], halo_in.at[0], halo_recv_sem.at[0]).wait()
        ext[0:half] = halo_in[0].astype(F32).reshape(half, depth, lanes)

    @pl.when(me == 0)
    def _():
        ext[0:half] = jnp.zeros((half, depth, lanes), F32)

    @pl.when(me < n - 1)
    def _():
        to_next(*halos).wait_send()
        pltpu.make_async_copy(halo_in.at[1], halo_in.at[1], halo_recv_sem.at[1]).wait()
        ext[half + x_rows :] = halo_in[1].astype(F32).reshape(half, depth, lanes)

    @pl.when(me == n - 1)
    def _():
        ext[half + x_rows :] = jnp.zeros((half, depth, lanes), F32)

    acc[...] = jnp.zeros(acc.shape, F32)
    copies = lanes // depth
    tall = copies * depth
    y_gap = lax.broadcasted_iota(jnp.int32, (lanes, lanes), 0) - lax.broadcasted_iota(jnp.int32, (lanes, lanes), 1)
    z_gap = (
        lax.rem(lax.broadcasted_iota(jnp.int32, (depth, tall), 1), depth)
        - lax.broadcasted_iota(jnp.int32, (depth, tall), 0)
    )
    same_block = (
        lax.broadcasted_iota(jnp.int32, (tall, tall), 0) // depth
        == lax.broadcasted_iota(jnp.int32, (tall, tall), 1) // depth
    )

    def total_of(ref, v, count):
        total = ref[v, 0]
        for k in range(1, count):
            total = total + ref[v, k]
        return total

    @pl.loop(0, views)
    def _(v):
        sum_x, sum_y, sum_z = total_of(px, v, taps), total_of(py, v, taps), total_of(pz, v, taps_z)
        scale_y = 1.0 / jnp.full((1, lanes), sum_y, F32)
        scale_z = 1.0 / jnp.full((1, tall), sum_z * sum_x, F32)
        fwd_y = jnp.zeros((lanes, lanes), F32)
        back_y = jnp.zeros((lanes, lanes), F32)
        for k in range(taps):
            fwd_y = jnp.where(y_gap == k - half, py[v, k], fwd_y)
            back_y = jnp.where(y_gap == half - k, py[v, k], back_y)
        fwd_z = jnp.zeros((depth, tall), F32)
        back_z = jnp.zeros((depth, tall), F32)
        for k in range(taps_z):
            fwd_z = jnp.where(z_gap == k - taps_z // 2, pz[v, k], fwd_z)
            back_z = jnp.where(z_gap == taps_z // 2 - k, pz[v, k], back_z)
        blocks_fwd = jnp.where(same_block, jnp.concatenate([fwd_z * scale_z] * copies, axis=0), 0.0)
        blocks_back = jnp.where(same_block, jnp.concatenate([back_z * scale_z] * copies, axis=0), 0.0)
        adj_z[v, 0], adj_z[v, 1] = split(blocks_back)
        adj_y[v, 0], adj_y[v, 1] = split(back_y * scale_y)
        z_parts = split(blocks_fwd)
        y_parts = split(fwd_y * scale_y)
        along_x = px[v, 0] * ext[0:x_rows]
        for k in range(1, taps):
            along_x = along_x + px[v, k] * ext[k : k + x_rows]
        along_x = along_x.reshape(lines, lanes)
        for part in range(lines // tall):
            piece = dot_split(z_parts, split(along_x[part * tall : (part + 1) * tall]))
            inverse[v, part * tall : (part + 1) * tall] = 1.0 / dot_split(split(piece), y_parts)

    last_lane = lax.broadcasted_iota(jnp.int32, (lines, lanes), 1) == lanes - 1
    arrived = pl.ds(0, slots - cap)

    @pl.loop(0, views)
    def _(v):
        pltpu.make_async_copy(recv.at[v, arrived], recv.at[v, arrived], line_recv_sem.at[v]).wait()
        line = dot(unpack[v], recv[v])
        following = jnp.where(last_lane, line, pltpu.roll(line, lanes - 1, 1))
        weight = interp[v].reshape(lines, lanes).astype(F32)
        quotient = (weight * line + (1.0 - weight) * following) * inverse[v]
        along_y = dot_split(split(quotient), (adj_y[v, 0], adj_y[v, 1]))
        z_parts = (adj_z[v, 0], adj_z[v, 1])
        corrected = jnp.concatenate(
            [dot_split(z_parts, split(along_y[p * tall : (p + 1) * tall])) for p in range(lines // tall)], axis=0
        ).reshape(x_rows, depth, lanes)
        for r in range(x_rows + 2 * half):
            total = acc[r]
            for k in range(taps):
                if 0 <= r - k < x_rows:
                    total = total + px[v, k] * corrected[r - k]
            acc[r] = total

    sum_out[0] = acc[0:half].reshape(edge, lanes).astype(BF16)
    sum_out[1] = acc[half + x_rows :].reshape(edge, lanes).astype(BF16)
    sums = (sum_out, sum_in, sum_send_sem, sum_recv_sem)

    @pl.when(me > 0)
    def _():
        to_prev(*sums).start()

    @pl.when(me < n - 1)
    def _():
        to_next(*sums).start()

    @pl.loop(0, views)
    def _(v):
        pltpu.make_async_copy(send.at[v, arrived], send.at[v, arrived], line_send_sem.at[v]).wait()

    out[...] = acc[half : half + x_rows]

    @pl.when(me > 0)
    def _():
        to_prev(*sums).wait_send()
        pltpu.make_async_copy(sum_in.at[0], sum_in.at[0], sum_recv_sem.at[0]).wait()
        out[0:half] = out[0:half] + sum_in[0].astype(F32).reshape(half, depth, lanes)

    @pl.when(me < n - 1)
    def _():
        to_next(*sums).wait_send()
        pltpu.make_async_copy(sum_in.at[1], sum_in.at[1], sum_recv_sem.at[1]).wait()
        out[x_rows - half :] = out[x_rows - half :] + sum_in[1].astype(F32).reshape(half, depth, lanes)


def body(estimate, observed, interp, source_rows, tissue, psf_x, psf_y, psf_z):
    n = lax.axis_size("tile")
    x_rows, depth, lanes = estimate.shape
    views = observed.shape[0]
    lines = x_rows * depth
    cap = 2 * lines // n
    slots = n * cap
    taps = psf_x.shape[1]
    half = taps // 2
    if cap % 16 or lanes % cap or n * views != lanes:
        return body_by_collectives(estimate, observed, interp, source_rows, tissue, psf_x, psf_y, psf_z)
    vmem = pl.BlockSpec(memory_space=pltpu.VMEM)
    smem = pl.BlockSpec(memory_space=pltpu.SMEM)
    edge = (2, half * depth, lanes)
    dma = pltpu.SemaphoreType.DMA
    running = pl.pallas_call(
        functools.partial(sweep_kernel, n),
        out_shape=jax.ShapeDtypeStruct(estimate.shape, F32),
        in_specs=[vmem] * 4 + [smem] * 3,
        out_specs=vmem,
        scratch_shapes=[
            pltpu.VMEM((x_rows + 2 * half, depth, lanes), F32),
            pltpu.VMEM(edge, BF16),
            pltpu.VMEM(edge, BF16),
            pltpu.VMEM((slots // lanes, views, lanes), F32),
            pltpu.VMEM((n, views, lanes), F32),
            pltpu.VMEM((lanes, n * views), F32),
            pltpu.VMEM((lines, lanes), F32),
            pltpu.VMEM((views, lines, slots), BF16),
            pltpu.VMEM((views, slots, lanes), BF16),
            pltpu.VMEM((views, slots, lanes), BF16),
            pltpu.VMEM((views, lines, lanes), F32),
            pltpu.VMEM((views, 2, lanes, lanes), BF16),
            pltpu.VMEM((views, 2, lanes, lanes), BF16),
            pltpu.VMEM((x_rows + 2 * half, depth, lanes), F32),
            pltpu.VMEM(edge, BF16),
            pltpu.VMEM(edge, BF16),
            dma((2,)), dma((2,)), dma, dma, dma((views,)), dma((views,)), dma((2,)), dma((2,)),
        ],
        compiler_params=pltpu.CompilerParams(
            collective_id=0, has_side_effects=True, vmem_limit_bytes=40 * 1024 * 1024
        ),
    )(estimate, observed, interp, source_rows.reshape(views, lines), psf_x, psf_y, psf_z)
    updated = estimate * running / views
    return jnp.where(tissue[:, None, None] == 1, updated, estimate)


def solution(mesh):
    return jax.shard_map(
        body,
        mesh=mesh,
        in_specs=(
            P(("slab", "tile"), None, None),
            P(None, ("slab", "tile"), None, None),
            P(None, ("slab", "tile"), None, None),
            P(None, ("slab", "tile"), None),
            P(("slab", "tile")),
            P(),
            P(),
            P(),
        ),
        out_specs=P(("slab", "tile"), None, None),
        check_vma=False,
    )
```

```python
import functools

import jax
import jax.numpy as jnp
from jax import lax
from jax.experimental import pallas as pl
from jax.experimental.pallas import tpu as pltpu
from jax.sharding import PartitionSpec as P


def extended_2(value, sides, width):
    for axis, dim in sides:
        size, length = (lax.axis_size(axis), value.shape[dim])
        up = [(i, (i + 1) % size) for i in range(size - 1)]
        down = [(j, i) for i, j in up]
        last = lax.slice_in_dim(value, length - width, length, axis=dim)
        first = lax.slice_in_dim(value, 0, width, axis=dim)
        before = lax.ppermute(last, axis, up)
        after = lax.ppermute(first, axis, down)
        value = jnp.concatenate([before, value, after], axis=dim)
    return value


def taps_matrix(coeffs, count):
    half_taps = coeffs.shape[0] // 2
    offsets = jnp.arange(count)[:, None] - jnp.arange(count)[None, :] + half_taps
    inside = (offsets >= 0) & (offsets < coeffs.shape[0])
    return jnp.where(inside, coeffs[jnp.clip(offsets, 0, coeffs.shape[0] - 1)], jnp.float32(0.0))


def forward_x(extended, coeffs, out_rows):
    result = coeffs[0] * extended[0:out_rows]
    for offset in range(1, coeffs.shape[0]):
        result = result + coeffs[offset] * extended[offset : offset + out_rows]
    return result


def adjoint_x(extended, coeffs, out_rows):
    half_taps = coeffs.shape[0] // 2
    result = jnp.zeros((out_rows,) + extended.shape[1:], jnp.float32)
    for offset in range(coeffs.shape[0]):
        start = 2 * half_taps - offset
        result = result + coeffs[offset] * extended[start : start + out_rows]
    return result


def forward_yz(volume, matrix_z, matrix_y):
    volume = jnp.einsum("xzy,zw->xwy", volume, matrix_z, precision=lax.Precision.HIGHEST)
    return jnp.einsum("xzy,yu->xzu", volume, matrix_y, precision=lax.Precision.HIGHEST)


def adjoint_yz(volume, matrix_z, matrix_y):
    volume = jnp.einsum("xzu,yu->xzy", volume, matrix_y, precision=lax.Precision.HIGHEST)
    return jnp.einsum("xwy,zw->xzy", volume, matrix_z, precision=lax.Precision.HIGHEST)


def body_by_collectives(estimate, observed, interp, source_rows, tissue, psf_x, psf_y, psf_z):
    tile_rows, depth_cells, lane_cells = estimate.shape
    view_count = observed.shape[0]
    tile_count = lax.axis_size("tile")
    line_count = tile_rows * depth_cells
    capacity = 2 * line_count // tile_count
    half_taps = psf_x.shape[1] // 2
    flat_obs = observed.reshape(view_count * line_count, lane_cells)
    owners = (source_rows // tile_rows).reshape(view_count, line_count)
    payload = (
        jnp.arange(view_count, dtype=jnp.int32)[:, None, None] * line_count
        + source_rows % tile_rows * depth_cells
        + jnp.arange(depth_cells, dtype=jnp.int32)[None, None, :]
    ).reshape(view_count, line_count)
    owner_hits = (
        owners[:, :, None] == jnp.arange(tile_count, dtype=jnp.int32)[None, None, :]
    ).astype(jnp.int32)
    slot_index = jnp.sum((jnp.cumsum(owner_hits, axis=1) - 1) * owner_hits, axis=2)
    view_column = jnp.broadcast_to(
        jnp.arange(view_count, dtype=jnp.int32)[:, None], (view_count, line_count)
    )
    requests = jnp.zeros((tile_count, view_count, capacity), jnp.int32)
    requests = requests.at[owners, view_column, slot_index].set(payload)
    returned = lax.all_to_all(
        flat_obs[lax.all_to_all(requests, "tile", split_axis=0, concat_axis=0, tiled=True)],
        "tile",
        split_axis=0,
        concat_axis=0,
        tiled=True,
    )
    gathered_lines = returned[owners, view_column, slot_index]
    extended = extended_2(estimate.astype(jnp.bfloat16), (("tile", 0),), half_taps).astype(
        estimate.dtype
    )
    running = jnp.zeros_like(estimate)
    for view in range(view_count):
        taps_x = psf_x[view] / jnp.sum(psf_x[view])
        taps_y = psf_y[view] / jnp.sum(psf_y[view])
        taps_z = psf_z[view] / jnp.sum(psf_z[view])
        matrix_z = taps_matrix(taps_z, depth_cells)
        matrix_y = taps_matrix(taps_y, lane_cells)
        view_lines = gathered_lines[view]
        source_line = view_lines.reshape(tile_rows, depth_cells, lane_cells).astype(jnp.float32)
        next_line = jnp.concatenate([source_line[..., 1:], source_line[..., -1:]], axis=2)
        weight = interp[view].astype(jnp.float32)
        joined_view = weight * source_line + (1.0 - weight) * next_line
        blurred = forward_yz(forward_x(extended, taps_x, tile_rows), matrix_z, matrix_y)
        quotient = joined_view / blurred
        corrected = adjoint_yz(quotient, matrix_z, matrix_y)
        corrected_band = extended_2(
            corrected.astype(jnp.bfloat16), (("tile", 0),), half_taps
        ).astype(corrected.dtype)
        running = running + adjoint_x(corrected_band, taps_x, tile_rows)
    updated = estimate * running / view_count
    return jnp.where(tissue[:, None, None] == 1, updated, estimate)


MESH = pl.DeviceIdType.MESH
RELAY_AFTER = 3
F32 = jnp.float32
BF16 = jnp.bfloat16


def split(value):
    high = value.astype(BF16)
    return high, (value - high.astype(F32)).astype(BF16)


def dot(left, right):
    return jnp.dot(left, right, preferred_element_type=F32)


def dot_split(left, right):
    return dot(left[0], right[0]) + dot(left[0], right[1]) + dot(left[1], right[0])


def one_hot(mask):
    return jnp.where(mask, 1.0, 0.0).astype(BF16)


def sweep_kernel(
    n, est_far, obs_far, interp_far, rows_far, tissue_far, px_far, py_far, pz_far, out,
    est, obs, interp, rows, tissue, px, py, pz, in_sem,
    ext, halo_out, halo_in, req_out, req_in, req_t, relay_in, relay_t, raw, raw_send, slot_t, unpack, send, recv,
    inverse, adj_z, adj_y, acc, sum_out, sum_in,
    halo_send_sem, halo_recv_sem, req_send_sem, req_recv_sem, line_send_sem, line_recv_sem,
    sum_send_sem, sum_recv_sem, relay_send_sem, relay_recv_sem, raw_send_sem, raw_recv_sem,
):
    x_rows, depth, lanes = est.shape
    views = obs.shape[0]
    lines = x_rows * depth
    cap = 2 * lines // n
    slots = n * cap
    per_block = lanes // cap
    taps = px.shape[1]
    taps_z = pz.shape[1]
    half = taps // 2
    edge = half * depth
    me = lax.axis_index("tile")
    side = n // 2
    place = lax.rem(me, side)
    base = me - place
    partner = lax.rem(me + side, n)
    partner_base = partner - place

    barrier = pltpu.get_barrier_semaphore()
    pairs = (
        (rows_far, rows), (est_far, est), (obs_far, obs), (interp_far, interp), (px_far, px), (py_far, py), (pz_far, pz),
        (tissue_far, tissue),
    )
    loads = [pltpu.make_async_copy(far, near, in_sem.at[i]) for i, (far, near) in enumerate(pairs)]
    for load in loads:
        load.start()

    @pl.loop(1, n)
    def _(j):
        pl.semaphore_signal(barrier, inc=1, device_id={"tile": lax.rem(me + j, n)}, device_id_type=MESH)

    loads[0].wait()
    wanted = jnp.concatenate([rows[:, x, :] for x in range(x_rows)], axis=1)
    owner = wanted // x_rows
    line_id = lax.broadcasted_iota(jnp.int32, (views, lines), 1)
    payload = ((wanted - owner * x_rows) * depth + lax.rem(line_id, depth)).astype(F32)
    hits = [jnp.where(owner == o, 1.0, 0.0) for o in range(n)]
    earlier = one_hot(
        lax.broadcasted_iota(jnp.int32, (lines, lines), 0) < lax.broadcasted_iota(jnp.int32, (lines, lines), 1)
    )
    rank = dot(jnp.concatenate(hits, axis=0).astype(BF16), earlier)
    slot = jnp.zeros((views, lines), F32)
    for o in range(n):
        slot = slot + hits[o] * (rank[o * views : (o + 1) * views] + float(o * cap))
    padded = jnp.concatenate([slot, jnp.zeros((lanes - views, lines), F32)], axis=0)
    slot_t[...] = padded.T

    view_row = lax.broadcasted_iota(jnp.int32, (views, lines), 0)
    slot_lane = lax.broadcasted_iota(jnp.int32, (lines, slots), 1).astype(F32)

    def request(v, total):
        column = pltpu.roll(slot_t[...], lax.rem(lanes - v, lanes), 1)[:, 0:1]
        chosen = one_hot(column == slot_lane)
        unpack[v] = chosen
        return total + dot(jnp.where(view_row == v, payload, 0.0).astype(BF16), chosen)

    requests = lax.fori_loop(0, views, request, jnp.zeros((views, slots), F32))
    for b in range(slots // lanes):
        req_out[b] = requests[:, b * lanes : (b + 1) * lanes]

    loads[1].wait()
    halo_out[0] = est[0:half].reshape(edge, lanes).astype(BF16)
    halo_out[1] = est[x_rows - half : x_rows].reshape(edge, lanes).astype(BF16)
    loads[2].wait()
    pl.semaphore_wait(barrier, n - 1)

    def halo_copy(source, target, send_sem, recv_sem, side, device):
        return pltpu.make_async_remote_copy(
            src_ref=source.at[side], dst_ref=target.at[1 - side],
            send_sem=send_sem.at[side], recv_sem=recv_sem.at[1 - side],
            device_id={"tile": device}, device_id_type=MESH,
        )

    def to_prev(source, target, send_sem, recv_sem):
        return halo_copy(source, target, send_sem, recv_sem, 0, lax.rem(me + n - 1, n))

    def to_next(source, target, send_sem, recv_sem):
        return halo_copy(source, target, send_sem, recv_sem, 1, lax.rem(me + 1, n))

    def request_copy(j):
        d = lax.rem(me + j, n)
        return pltpu.make_async_remote_copy(
            src_ref=req_out.at[d // per_block], dst_ref=req_in.at[me],
            send_sem=req_send_sem, recv_sem=req_recv_sem,
            device_id={"tile": d}, device_id_type=MESH,
        )

    def relay_request_copy(j):
        d = base + lax.rem(place + j, side)
        return pltpu.make_async_remote_copy(
            src_ref=req_out.at[lax.rem(d + side, n) // per_block], dst_ref=relay_in.at[place],
            send_sem=relay_send_sem, recv_sem=relay_recv_sem,
            device_id={"tile": d}, device_id_type=MESH,
        )

    raw_copy = pltpu.make_async_remote_copy(
        src_ref=obs.at[0], dst_ref=raw, send_sem=raw_send_sem, recv_sem=raw_recv_sem,
        device_id={"tile": partner}, device_id_type=MESH,
    )

    @pl.loop(1, n)
    def _(j):
        request_copy(j).start()

    raw_copy.start()

    @pl.loop(1, side)
    def _(j):
        relay_request_copy(j).start()

    halos = (halo_out, halo_in, halo_send_sem, halo_recv_sem)

    @pl.when(me > 0)
    def _():
        to_prev(*halos).start()

    @pl.when(me < n - 1)
    def _():
        to_next(*halos).start()

    req_in[me] = req_out[me // per_block]
    ahead = pl.ds(0, n - 1)
    pltpu.make_async_copy(req_in.at[ahead], req_in.at[ahead], req_recv_sem).wait()
    pltpu.make_async_copy(req_in.at[ahead], req_in.at[ahead], req_send_sem).wait()

    req_t[...] = req_in[...].reshape(n * views, lanes).T
    mine = req_t[pl.ds(lax.rem(me, per_block) * cap, cap), :]
    line_lane = lax.broadcasted_iota(jnp.int32, (cap, lines), 1).astype(F32)
    own = pl.ds(pl.multiple_of(me * cap, cap), cap)

    def line_copy(v, source, target, d):
        return pltpu.make_async_remote_copy(
            src_ref=source, dst_ref=recv.at[v, target],
            send_sem=line_send_sem.at[v], recv_sem=line_recv_sem.at[v],
            device_id={"tile": d}, device_id_type=MESH,
        )

    def chunk(index):
        return pl.ds(pl.multiple_of(index * cap, cap), cap)

    def pack(v):
        turned = pltpu.roll(mine, lax.rem(lanes - v, lanes), 1)
        chosen = jnp.concatenate(
            [one_hot(turned[:, d * views : d * views + 1] == line_lane) for d in range(n)], axis=0
        )
        send[v] = dot(chosen, obs[v].reshape(lines, lanes)).astype(BF16)

    def send_view(v):
        pack(v)

        @pl.loop(0, side)
        def _(j):
            d = partner_base + lax.rem(place + j, side)
            line_copy(v, send.at[v, chunk(d)], own, d).start()

        @pl.loop(1, side)
        def _(j):
            d = base + lax.rem(place + j, side)
            line_copy(v, send.at[v, chunk(d)], own, d).start()

        recv[v, own] = send[v, own]

    pl.loop(1, RELAY_AFTER)(send_view)

    pltpu.make_async_copy(relay_in.at[pl.ds(0, side - 1)], relay_in.at[pl.ds(0, side - 1)], relay_recv_sem).wait()
    pltpu.make_async_copy(relay_in.at[pl.ds(0, side - 1)], relay_in.at[pl.ds(0, side - 1)], relay_send_sem).wait()
    relay_in[place] = req_out[partner // per_block]
    relay_t[...] = relay_in[...].reshape(side * views, lanes).T
    others = relay_t[pl.ds(lax.rem(partner, per_block) * cap, cap), :]
    chosen_raw = jnp.concatenate(
        [one_hot(others[:, d * views : d * views + 1] == line_lane) for d in range(side)], axis=0
    )
    pack(0)
    raw_copy.wait()
    raw_send[...] = dot(chosen_raw, raw[...].reshape(lines, lanes)).astype(BF16)

    @pl.loop(1, side)
    def _(j):
        there = lax.rem(place + j, side)
        line_copy(0, raw_send.at[chunk(there)], chunk(partner), base + there).start()
        line_copy(0, send.at[0, chunk(base + there)], own, base + there).start()

    recv[0, own] = send[0, own]
    recv[0, chunk(partner)] = raw_send[chunk(place)]
    pl.loop(RELAY_AFTER, views)(send_view)

    ext[half : half + x_rows] = est[...]

    @pl.when(me > 0)
    def _():
        to_prev(*halos).wait_send()
        pltpu.make_async_copy(halo_in.at[0], halo_in.at[0], halo_recv_sem.at[0]).wait()
        ext[0:half] = halo_in[0].astype(F32).reshape(half, depth, lanes)

    @pl.when(me == 0)
    def _():
        ext[0:half] = jnp.zeros((half, depth, lanes), F32)

    @pl.when(me < n - 1)
    def _():
        to_next(*halos).wait_send()
        pltpu.make_async_copy(halo_in.at[1], halo_in.at[1], halo_recv_sem.at[1]).wait()
        ext[half + x_rows :] = halo_in[1].astype(F32).reshape(half, depth, lanes)

    @pl.when(me == n - 1)
    def _():
        ext[half + x_rows :] = jnp.zeros((half, depth, lanes), F32)

    for load in loads[3:]:
        load.wait()
    acc[...] = jnp.zeros(acc.shape, F32)
    copies = lanes // depth
    tall = copies * depth
    y_gap = lax.broadcasted_iota(jnp.int32, (lanes, lanes), 0) - lax.broadcasted_iota(jnp.int32, (lanes, lanes), 1)
    z_gap = (
        lax.rem(lax.broadcasted_iota(jnp.int32, (depth, tall), 1), depth)
        - lax.broadcasted_iota(jnp.int32, (depth, tall), 0)
    )
    same_block = (
        lax.broadcasted_iota(jnp.int32, (tall, tall), 0) // depth
        == lax.broadcasted_iota(jnp.int32, (tall, tall), 1) // depth
    )

    def total_of(ref, v, count):
        total = ref[v, 0]
        for k in range(1, count):
            total = total + ref[v, k]
        return total

    @pl.loop(0, views)
    def _(v):
        sum_x, sum_y, sum_z = total_of(px, v, taps), total_of(py, v, taps), total_of(pz, v, taps_z)
        scale_y = 1.0 / jnp.full((1, lanes), sum_y, F32)
        scale_z = 1.0 / jnp.full((1, tall), sum_z * sum_x, F32)
        fwd_y = jnp.zeros((lanes, lanes), F32)
        back_y = jnp.zeros((lanes, lanes), F32)
        for k in range(taps):
            fwd_y = jnp.where(y_gap == k - half, py[v, k], fwd_y)
            back_y = jnp.where(y_gap == half - k, py[v, k], back_y)
        fwd_z = jnp.zeros((depth, tall), F32)
        back_z = jnp.zeros((depth, tall), F32)
        for k in range(taps_z):
            fwd_z = jnp.where(z_gap == k - taps_z // 2, pz[v, k], fwd_z)
            back_z = jnp.where(z_gap == taps_z // 2 - k, pz[v, k], back_z)
        blocks_fwd = jnp.where(same_block, jnp.concatenate([fwd_z * scale_z] * copies, axis=0), 0.0)
        blocks_back = jnp.where(same_block, jnp.concatenate([back_z * scale_z] * copies, axis=0), 0.0)
        adj_z[v, 0], adj_z[v, 1] = split(blocks_back)
        adj_y[v, 0], adj_y[v, 1] = split(back_y * scale_y)
        z_parts = split(blocks_fwd)
        y_parts = split(fwd_y * scale_y)
        along_x = px[v, 0] * ext[0:x_rows]
        for k in range(1, taps):
            along_x = along_x + px[v, k] * ext[k : k + x_rows]
        along_x = along_x.reshape(lines, lanes)
        for part in range(lines // tall):
            piece = dot_split(z_parts, split(along_x[part * tall : (part + 1) * tall]))
            inverse[v, part * tall : (part + 1) * tall] = 1.0 / dot_split(split(piece), y_parts)

    last_lane = lax.broadcasted_iota(jnp.int32, (lines, lanes), 1) == lanes - 1
    arrived = pl.ds(0, slots - cap)

    relayed = pl.ds(0, 2 * (side - 1) * cap)

    @pl.loop(0, views)
    def _(turn):
        v = jnp.where(turn < RELAY_AFTER - 1, turn + 1, jnp.where(turn == RELAY_AFTER - 1, 0, turn))

        @pl.when(v == 0)
        def _():
            pltpu.make_async_copy(recv.at[0, relayed], recv.at[0, relayed], line_recv_sem.at[0]).wait()

        @pl.when(v > 0)
        def _():
            pltpu.make_async_copy(recv.at[v, arrived], recv.at[v, arrived], line_recv_sem.at[v]).wait()

        line = dot(unpack[v], recv[v])
        following = jnp.where(last_lane, line, pltpu.roll(line, lanes - 1, 1))
        weight = interp[v].reshape(lines, lanes).astype(F32)
        quotient = (weight * line + (1.0 - weight) * following) * inverse[v]
        along_y = dot_split(split(quotient), (adj_y[v, 0], adj_y[v, 1]))
        z_parts = (adj_z[v, 0], adj_z[v, 1])
        corrected = jnp.concatenate(
            [dot_split(z_parts, split(along_y[p * tall : (p + 1) * tall])) for p in range(lines // tall)], axis=0
        ).reshape(x_rows, depth, lanes)
        for r in range(x_rows + 2 * half):
            total = acc[r]
            for k in range(taps):
                if 0 <= r - k < x_rows:
                    total = total + px[v, k] * corrected[r - k]
            acc[r] = total

    sum_out[0] = acc[0:half].reshape(edge, lanes).astype(BF16)
    sum_out[1] = acc[half + x_rows :].reshape(edge, lanes).astype(BF16)
    sums = (sum_out, sum_in, sum_send_sem, sum_recv_sem)

    @pl.when(me > 0)
    def _():
        to_prev(*sums).start()

    @pl.when(me < n - 1)
    def _():
        to_next(*sums).start()

    pltpu.make_async_copy(send.at[0, relayed], send.at[0, relayed], line_send_sem.at[0]).wait()

    @pl.loop(1, views)
    def _(v):
        pltpu.make_async_copy(send.at[v, arrived], send.at[v, arrived], line_send_sem.at[v]).wait()

    @pl.when(me > 0)
    def _():
        to_prev(*sums).wait_send()
        pltpu.make_async_copy(sum_in.at[0], sum_in.at[0], sum_recv_sem.at[0]).wait()
        acc[half : 2 * half] = acc[half : 2 * half] + sum_in[0].astype(F32).reshape(half, depth, lanes)

    @pl.when(me < n - 1)
    def _():
        to_next(*sums).wait_send()
        pltpu.make_async_copy(sum_in.at[1], sum_in.at[1], sum_recv_sem.at[1]).wait()
        acc[x_rows : x_rows + half] = acc[x_rows : x_rows + half] + sum_in[1].astype(F32).reshape(half, depth, lanes)

    for x in range(x_rows):
        updated = est[x] * acc[half + x] * (1.0 / views)
        out[x] = jnp.where(jnp.full((depth, lanes), tissue[x]) == 1, updated, est[x])


def body(estimate, observed, interp, source_rows, tissue, psf_x, psf_y, psf_z):
    n = lax.axis_size("tile")
    x_rows, depth, lanes = estimate.shape
    views = observed.shape[0]
    lines = x_rows * depth
    cap = 2 * lines // n
    slots = n * cap
    taps = psf_x.shape[1]
    half = taps // 2
    if cap % 16 or lanes % cap or n * views != lanes:
        return body_by_collectives(estimate, observed, interp, source_rows, tissue, psf_x, psf_y, psf_z)
    vmem = pl.BlockSpec(memory_space=pltpu.VMEM)
    edge = (2, half * depth, lanes)
    dma = pltpu.SemaphoreType.DMA
    return pl.pallas_call(
        functools.partial(sweep_kernel, n),
        out_shape=jax.ShapeDtypeStruct(estimate.shape, F32),
        in_specs=[pl.BlockSpec(memory_space=pl.ANY)] * 8,
        out_specs=vmem,
        scratch_shapes=[
            pltpu.VMEM(estimate.shape, F32),
            pltpu.VMEM(observed.shape, BF16),
            pltpu.VMEM(interp.shape, BF16),
            pltpu.VMEM(source_rows.shape, jnp.int32),
            pltpu.SMEM(tissue.shape, jnp.int32),
            pltpu.SMEM(psf_x.shape, F32),
            pltpu.SMEM(psf_y.shape, F32),
            pltpu.SMEM(psf_z.shape, F32),
            dma((8,)),
            pltpu.VMEM((x_rows + 2 * half, depth, lanes), F32),
            pltpu.VMEM(edge, BF16),
            pltpu.VMEM(edge, BF16),
            pltpu.VMEM((slots // lanes, views, lanes), F32),
            pltpu.VMEM((n, views, lanes), F32),
            pltpu.VMEM((lanes, n * views), F32),
            pltpu.VMEM((n // 2, views, lanes), F32),
            pltpu.VMEM((lanes, n // 2 * views), F32),
            pltpu.VMEM((x_rows, depth, lanes), BF16),
            pltpu.VMEM((n // 2 * cap, lanes), BF16),
            pltpu.VMEM((lines, lanes), F32),
            pltpu.VMEM((views, lines, slots), BF16),
            pltpu.VMEM((views, slots, lanes), BF16),
            pltpu.VMEM((views, slots, lanes), BF16),
            pltpu.VMEM((views, lines, lanes), F32),
            pltpu.VMEM((views, 2, lanes, lanes), BF16),
            pltpu.VMEM((views, 2, lanes, lanes), BF16),
            pltpu.VMEM((x_rows + 2 * half, depth, lanes), F32),
            pltpu.VMEM(edge, BF16),
            pltpu.VMEM(edge, BF16),
            dma((2,)), dma((2,)), dma, dma, dma((views,)), dma((views,)), dma((2,)), dma((2,)), dma, dma, dma, dma,
        ],
        compiler_params=pltpu.CompilerParams(
            collective_id=0, has_side_effects=True, vmem_limit_bytes=60 * 1024 * 1024
        ),
    )(estimate, observed, interp, source_rows, tissue, psf_x, psf_y, psf_z)


def solution(mesh):
    return jax.shard_map(
        body,
        mesh=mesh,
        in_specs=(
            P(("slab", "tile"), None, None),
            P(None, ("slab", "tile"), None, None),
            P(None, ("slab", "tile"), None, None),
            P(None, ("slab", "tile"), None),
            P(("slab", "tile")),
            P(),
            P(),
            P(),
        ),
        out_specs=P(("slab", "tile"), None, None),
        check_vma=False,
    )
```

```python
import functools

import jax
import jax.numpy as jnp
from jax import lax
from jax.experimental import pallas as pl
from jax.experimental.pallas import tpu as pltpu
from jax.sharding import PartitionSpec as P


def extended_2(value, sides, width):
    for axis, dim in sides:
        size, length = (lax.axis_size(axis), value.shape[dim])
        up = [(i, (i + 1) % size) for i in range(size - 1)]
        down = [(j, i) for i, j in up]
        last = lax.slice_in_dim(value, length - width, length, axis=dim)
        first = lax.slice_in_dim(value, 0, width, axis=dim)
        before = lax.ppermute(last, axis, up)
        after = lax.ppermute(first, axis, down)
        value = jnp.concatenate([before, value, after], axis=dim)
    return value


def taps_matrix(coeffs, count):
    half_taps = coeffs.shape[0] // 2
    offsets = jnp.arange(count)[:, None] - jnp.arange(count)[None, :] + half_taps
    inside = (offsets >= 0) & (offsets < coeffs.shape[0])
    return jnp.where(inside, coeffs[jnp.clip(offsets, 0, coeffs.shape[0] - 1)], jnp.float32(0.0))


def forward_x(extended, coeffs, out_rows):
    result = coeffs[0] * extended[0:out_rows]
    for offset in range(1, coeffs.shape[0]):
        result = result + coeffs[offset] * extended[offset : offset + out_rows]
    return result


def adjoint_x(extended, coeffs, out_rows):
    half_taps = coeffs.shape[0] // 2
    result = jnp.zeros((out_rows,) + extended.shape[1:], jnp.float32)
    for offset in range(coeffs.shape[0]):
        start = 2 * half_taps - offset
        result = result + coeffs[offset] * extended[start : start + out_rows]
    return result


def forward_yz(volume, matrix_z, matrix_y):
    volume = jnp.einsum("xzy,zw->xwy", volume, matrix_z, precision=lax.Precision.HIGHEST)
    return jnp.einsum("xzy,yu->xzu", volume, matrix_y, precision=lax.Precision.HIGHEST)


def adjoint_yz(volume, matrix_z, matrix_y):
    volume = jnp.einsum("xzu,yu->xzy", volume, matrix_y, precision=lax.Precision.HIGHEST)
    return jnp.einsum("xwy,zw->xzy", volume, matrix_z, precision=lax.Precision.HIGHEST)


def body_by_collectives(estimate, observed, interp, source_rows, tissue, psf_x, psf_y, psf_z):
    tile_rows, depth_cells, lane_cells = estimate.shape
    view_count = observed.shape[0]
    tile_count = lax.axis_size("tile")
    line_count = tile_rows * depth_cells
    capacity = 2 * line_count // tile_count
    half_taps = psf_x.shape[1] // 2
    flat_obs = observed.reshape(view_count * line_count, lane_cells)
    owners = (source_rows // tile_rows).reshape(view_count, line_count)
    payload = (
        jnp.arange(view_count, dtype=jnp.int32)[:, None, None] * line_count
        + source_rows % tile_rows * depth_cells
        + jnp.arange(depth_cells, dtype=jnp.int32)[None, None, :]
    ).reshape(view_count, line_count)
    owner_hits = (
        owners[:, :, None] == jnp.arange(tile_count, dtype=jnp.int32)[None, None, :]
    ).astype(jnp.int32)
    slot_index = jnp.sum((jnp.cumsum(owner_hits, axis=1) - 1) * owner_hits, axis=2)
    view_column = jnp.broadcast_to(
        jnp.arange(view_count, dtype=jnp.int32)[:, None], (view_count, line_count)
    )
    requests = jnp.zeros((tile_count, view_count, capacity), jnp.int32)
    requests = requests.at[owners, view_column, slot_index].set(payload)
    returned = lax.all_to_all(
        flat_obs[lax.all_to_all(requests, "tile", split_axis=0, concat_axis=0, tiled=True)],
        "tile",
        split_axis=0,
        concat_axis=0,
        tiled=True,
    )
    gathered_lines = returned[owners, view_column, slot_index]
    extended = extended_2(estimate.astype(jnp.bfloat16), (("tile", 0),), half_taps).astype(
        estimate.dtype
    )
    running = jnp.zeros_like(estimate)
    for view in range(view_count):
        taps_x = psf_x[view] / jnp.sum(psf_x[view])
        taps_y = psf_y[view] / jnp.sum(psf_y[view])
        taps_z = psf_z[view] / jnp.sum(psf_z[view])
        matrix_z = taps_matrix(taps_z, depth_cells)
        matrix_y = taps_matrix(taps_y, lane_cells)
        view_lines = gathered_lines[view]
        source_line = view_lines.reshape(tile_rows, depth_cells, lane_cells).astype(jnp.float32)
        next_line = jnp.concatenate([source_line[..., 1:], source_line[..., -1:]], axis=2)
        weight = interp[view].astype(jnp.float32)
        joined_view = weight * source_line + (1.0 - weight) * next_line
        blurred = forward_yz(forward_x(extended, taps_x, tile_rows), matrix_z, matrix_y)
        quotient = joined_view / blurred
        corrected = adjoint_yz(quotient, matrix_z, matrix_y)
        corrected_band = extended_2(
            corrected.astype(jnp.bfloat16), (("tile", 0),), half_taps
        ).astype(corrected.dtype)
        running = running + adjoint_x(corrected_band, taps_x, tile_rows)
    updated = estimate * running / view_count
    return jnp.where(tissue[:, None, None] == 1, updated, estimate)


MESH = pl.DeviceIdType.MESH
RELAY_AFTER = 3
F32 = jnp.float32
BF16 = jnp.bfloat16


def split(value):
    high = value.astype(BF16)
    return high, (value - high.astype(F32)).astype(BF16)


def dot(left, right):
    return jnp.dot(left, right, preferred_element_type=F32)


def dot_split(left, right):
    return dot(left[0], right[0]) + dot(left[0], right[1]) + dot(left[1], right[0])


def one_hot(mask):
    return jnp.where(mask, 1.0, 0.0).astype(BF16)


def sweep_kernel(
    n, est_far, obs_far, interp_far, rows_far, tissue_far, px_far, py_far, pz_far, out,
    est, obs, interp, rows, tissue, px, py, pz, in_sem,
    ext, halo_out, halo_in, req_out, req_in, req_t, relay_in, relay_t, raw, raw_send, slot_t, unpack, send, recv,
    inverse, adj_z, adj_y, acc, sum_out, sum_in,
    halo_send_sem, halo_recv_sem, req_send_sem, req_recv_sem, line_send_sem, line_recv_sem,
    sum_send_sem, sum_recv_sem, relay_send_sem, relay_recv_sem, raw_send_sem, raw_recv_sem,
):
    x_rows, depth, lanes = est.shape
    views = obs.shape[0]
    lines = x_rows * depth
    cap = 2 * lines // n
    slots = n * cap
    per_block = lanes // cap
    groups = views // per_block
    taps = px.shape[1]
    taps_z = pz.shape[1]
    half = taps // 2
    edge = half * depth
    me = lax.axis_index("tile")
    side = n // 2
    place = lax.rem(me, side)
    base = me - place
    partner = lax.rem(me + side, n)
    partner_base = partner - place

    barrier = pltpu.get_barrier_semaphore()
    pairs = (
        (rows_far, rows), (est_far, est), (obs_far, obs), (interp_far, interp), (px_far, px), (py_far, py), (pz_far, pz),
        (tissue_far, tissue),
    )
    loads = [pltpu.make_async_copy(far, near, in_sem.at[i]) for i, (far, near) in enumerate(pairs)]
    for load in loads:
        load.start()

    @pl.loop(1, n)
    def _(j):
        pl.semaphore_signal(barrier, inc=1, device_id={"tile": lax.rem(me + j, n)}, device_id_type=MESH)

    loads[0].wait()
    wanted = jnp.concatenate([rows[:, x, :] for x in range(x_rows)], axis=1)
    owner = wanted // x_rows
    line_id = lax.broadcasted_iota(jnp.int32, (views, lines), 1)
    payload = ((wanted - owner * x_rows) * depth + lax.rem(line_id, depth)).astype(F32)
    hits = [jnp.where(owner == o, 1.0, 0.0) for o in range(n)]
    earlier = one_hot(
        lax.broadcasted_iota(jnp.int32, (lines, lines), 0) < lax.broadcasted_iota(jnp.int32, (lines, lines), 1)
    )
    ranks = dot(jnp.concatenate(hits, axis=0).astype(BF16), earlier)
    rank = jnp.zeros((views, lines), F32)
    offset = jnp.zeros((views, lines), F32)
    for o in range(n):
        rank = rank + hits[o] * ranks[o * views : (o + 1) * views]
        offset = offset + hits[o] * float(o * cap)
    spot = rank + (lax.rem(lax.broadcasted_iota(jnp.int32, (views, lines), 0), per_block) * cap).astype(F32)
    empty = jnp.zeros((lanes - 2 * views, lines), F32)
    columns = jnp.concatenate([spot, rank + offset, empty], axis=0).T
    slot_t[...] = columns
    owner_id = lax.broadcasted_iota(jnp.int32, (n, lines), 0)
    lane_id = lax.broadcasted_iota(jnp.int32, (lines, lanes), 1).astype(F32)
    for g in range(groups):
        total = jnp.zeros((n, lanes), F32)
        for v in range(g * per_block, (g + 1) * per_block):
            theirs = jnp.where(owner[v : v + 1] == owner_id, payload[v : v + 1], 0.0).astype(BF16)
            total = total + dot(theirs, one_hot(columns[:, v : v + 1] == lane_id))
        req_out[:, g, :] = total

    loads[1].wait()
    halo_out[0] = est[0:half].reshape(edge, lanes).astype(BF16)
    halo_out[1] = est[x_rows - half : x_rows].reshape(edge, lanes).astype(BF16)
    loads[2].wait()
    pl.semaphore_wait(barrier, n - 1)

    def halo_copy(source, target, send_sem, recv_sem, side, device):
        return pltpu.make_async_remote_copy(
            src_ref=source.at[side], dst_ref=target.at[1 - side],
            send_sem=send_sem.at[side], recv_sem=recv_sem.at[1 - side],
            device_id={"tile": device}, device_id_type=MESH,
        )

    def to_prev(source, target, send_sem, recv_sem):
        return halo_copy(source, target, send_sem, recv_sem, 0, lax.rem(me + n - 1, n))

    def to_next(source, target, send_sem, recv_sem):
        return halo_copy(source, target, send_sem, recv_sem, 1, lax.rem(me + 1, n))

    def request_copy(j):
        d = lax.rem(me + j, n)
        return pltpu.make_async_remote_copy(
            src_ref=req_out.at[d], dst_ref=req_in.at[me],
            send_sem=req_send_sem, recv_sem=req_recv_sem,
            device_id={"tile": d}, device_id_type=MESH,
        )

    def relay_request_copy(j):
        d = base + lax.rem(place + j, side)
        return pltpu.make_async_remote_copy(
            src_ref=req_out.at[lax.rem(d + side, n)], dst_ref=relay_in.at[place],
            send_sem=relay_send_sem, recv_sem=relay_recv_sem,
            device_id={"tile": d}, device_id_type=MESH,
        )

    raw_copy = pltpu.make_async_remote_copy(
        src_ref=obs.at[0], dst_ref=raw, send_sem=raw_send_sem, recv_sem=raw_recv_sem,
        device_id={"tile": partner}, device_id_type=MESH,
    )

    @pl.loop(1, n)
    def _(j):
        request_copy(j).start()

    raw_copy.start()

    @pl.loop(1, side)
    def _(j):
        relay_request_copy(j).start()

    halos = (halo_out, halo_in, halo_send_sem, halo_recv_sem)

    @pl.when(me > 0)
    def _():
        to_prev(*halos).start()

    @pl.when(me < n - 1)
    def _():
        to_next(*halos).start()

    def turned_requests(ref, count):
        parts = [ref[:, g, :] for g in range(groups)]
        return jnp.concatenate(parts + [jnp.zeros((lanes - groups * count, lanes), F32)], axis=0).T

    req_in[me] = req_out[me]
    ahead = pl.ds(0, n - 1)
    pltpu.make_async_copy(req_in.at[ahead], req_in.at[ahead], req_recv_sem).wait()
    pltpu.make_async_copy(req_in.at[ahead], req_in.at[ahead], req_send_sem).wait()

    req_t[...] = turned_requests(req_in, n)
    line_lane = lax.broadcasted_iota(jnp.int32, (cap, lines), 1).astype(F32)
    own = pl.ds(pl.multiple_of(me * cap, cap), cap)

    def line_copy(v, source, target, d):
        return pltpu.make_async_remote_copy(
            src_ref=source, dst_ref=recv.at[v, target],
            send_sem=line_send_sem.at[v], recv_sem=line_recv_sem.at[v],
            device_id={"tile": d}, device_id_type=MESH,
        )

    def chunk(index):
        return pl.ds(pl.multiple_of(index * cap, cap), cap)

    def pack(v):
        group = v // per_block
        lines_of_view = req_t[pl.ds(pl.multiple_of((v - group * per_block) * cap, cap), cap), :]
        turned = pltpu.roll(lines_of_view, lax.rem(lanes - group * n, lanes), 1)
        chosen = jnp.concatenate([one_hot(turned[:, d : d + 1] == line_lane) for d in range(n)], axis=0)
        send[v] = dot(chosen, obs[v].reshape(lines, lanes)).astype(BF16)

    def send_view(v):
        pack(v)

        @pl.loop(0, side)
        def _(j):
            d = partner_base + lax.rem(place + j, side)
            line_copy(v, send.at[v, chunk(d)], own, d).start()

        @pl.loop(1, side)
        def _(j):
            d = base + lax.rem(place + j, side)
            line_copy(v, send.at[v, chunk(d)], own, d).start()

        recv[v, own] = send[v, own]

    pl.loop(1, RELAY_AFTER)(send_view)

    pltpu.make_async_copy(relay_in.at[pl.ds(0, side - 1)], relay_in.at[pl.ds(0, side - 1)], relay_recv_sem).wait()
    pltpu.make_async_copy(relay_in.at[pl.ds(0, side - 1)], relay_in.at[pl.ds(0, side - 1)], relay_send_sem).wait()
    relay_in[place] = req_out[partner]
    relay_t[...] = turned_requests(relay_in, side)
    others = relay_t[0:cap, :]
    chosen_raw = jnp.concatenate([one_hot(others[:, d : d + 1] == line_lane) for d in range(side)], axis=0)
    pack(0)
    raw_copy.wait()
    raw_send[...] = dot(chosen_raw, raw[...].reshape(lines, lanes)).astype(BF16)

    @pl.loop(1, side)
    def _(j):
        there = lax.rem(place + j, side)
        line_copy(0, raw_send.at[chunk(there)], chunk(partner), base + there).start()
        line_copy(0, send.at[0, chunk(base + there)], own, base + there).start()

    recv[0, own] = send[0, own]
    recv[0, chunk(partner)] = raw_send[chunk(place)]
    pl.loop(RELAY_AFTER, views)(send_view)

    ext[half : half + x_rows] = est[...]

    @pl.when(me > 0)
    def _():
        to_prev(*halos).wait_send()
        pltpu.make_async_copy(halo_in.at[0], halo_in.at[0], halo_recv_sem.at[0]).wait()
        ext[0:half] = halo_in[0].astype(F32).reshape(half, depth, lanes)

    @pl.when(me == 0)
    def _():
        ext[0:half] = jnp.zeros((half, depth, lanes), F32)

    @pl.when(me < n - 1)
    def _():
        to_next(*halos).wait_send()
        pltpu.make_async_copy(halo_in.at[1], halo_in.at[1], halo_recv_sem.at[1]).wait()
        ext[half + x_rows :] = halo_in[1].astype(F32).reshape(half, depth, lanes)

    @pl.when(me == n - 1)
    def _():
        ext[half + x_rows :] = jnp.zeros((half, depth, lanes), F32)

    for load in loads[3:]:
        load.wait()
    acc[...] = jnp.zeros(acc.shape, F32)
    copies = lanes // depth
    tall = copies * depth
    y_gap = lax.broadcasted_iota(jnp.int32, (lanes, lanes), 0) - lax.broadcasted_iota(jnp.int32, (lanes, lanes), 1)
    z_gap = (
        lax.rem(lax.broadcasted_iota(jnp.int32, (depth, tall), 1), depth)
        - lax.broadcasted_iota(jnp.int32, (depth, tall), 0)
    )
    same_block = (
        lax.broadcasted_iota(jnp.int32, (tall, tall), 0) // depth
        == lax.broadcasted_iota(jnp.int32, (tall, tall), 1) // depth
    )

    def total_of(ref, v, count):
        total = ref[v, 0]
        for k in range(1, count):
            total = total + ref[v, k]
        return total

    slot_lane = lax.broadcasted_iota(jnp.int32, (lines, slots), 1).astype(F32)

    @pl.loop(0, views)
    def _(v):
        unpack[v] = one_hot(pltpu.roll(slot_t[...], lax.rem(lanes - views - v, lanes), 1)[:, 0:1] == slot_lane)
        sum_x, sum_y, sum_z = total_of(px, v, taps), total_of(py, v, taps), total_of(pz, v, taps_z)
        scale_y = 1.0 / jnp.full((1, lanes), sum_y, F32)
        scale_z = 1.0 / jnp.full((1, tall), sum_z * sum_x, F32)
        fwd_y = jnp.zeros((lanes, lanes), F32)
        back_y = jnp.zeros((lanes, lanes), F32)
        for k in range(taps):
            fwd_y = jnp.where(y_gap == k - half, py[v, k], fwd_y)
            back_y = jnp.where(y_gap == half - k, py[v, k], back_y)
        fwd_z = jnp.zeros((depth, tall), F32)
        back_z = jnp.zeros((depth, tall), F32)
        for k in range(taps_z):
            fwd_z = jnp.where(z_gap == k - taps_z // 2, pz[v, k], fwd_z)
            back_z = jnp.where(z_gap == taps_z // 2 - k, pz[v, k], back_z)
        blocks_fwd = jnp.where(same_block, jnp.concatenate([fwd_z * scale_z] * copies, axis=0), 0.0)
        blocks_back = jnp.where(same_block, jnp.concatenate([back_z * scale_z] * copies, axis=0), 0.0)
        adj_z[v, 0], adj_z[v, 1] = split(blocks_back)
        adj_y[v, 0], adj_y[v, 1] = split(back_y * scale_y)
        z_parts = split(blocks_fwd)
        y_parts = split(fwd_y * scale_y)
        along_x = px[v, 0] * ext[0:x_rows]
        for k in range(1, taps):
            along_x = along_x + px[v, k] * ext[k : k + x_rows]
        along_x = along_x.reshape(lines, lanes)
        for part in range(lines // tall):
            piece = dot_split(z_parts, split(along_x[part * tall : (part + 1) * tall]))
            inverse[v, part * tall : (part + 1) * tall] = 1.0 / dot_split(split(piece), y_parts)

    last_lane = lax.broadcasted_iota(jnp.int32, (lines, lanes), 1) == lanes - 1
    arrived = pl.ds(0, slots - cap)

    relayed = pl.ds(0, 2 * (side - 1) * cap)

    @pl.loop(0, views)
    def _(turn):
        v = jnp.where(turn < RELAY_AFTER - 1, turn + 1, jnp.where(turn == RELAY_AFTER - 1, 0, turn))

        @pl.when(v == 0)
        def _():
            pltpu.make_async_copy(recv.at[0, relayed], recv.at[0, relayed], line_recv_sem.at[0]).wait()

        @pl.when(v > 0)
        def _():
            pltpu.make_async_copy(recv.at[v, arrived], recv.at[v, arrived], line_recv_sem.at[v]).wait()

        line = dot(unpack[v], recv[v])
        following = jnp.where(last_lane, line, pltpu.roll(line, lanes - 1, 1))
        weight = interp[v].reshape(lines, lanes).astype(F32)
        quotient = (weight * line + (1.0 - weight) * following) * inverse[v]
        along_y = dot_split(split(quotient), (adj_y[v, 0], adj_y[v, 1]))
        z_parts = (adj_z[v, 0], adj_z[v, 1])
        corrected = jnp.concatenate(
            [dot_split(z_parts, split(along_y[p * tall : (p + 1) * tall])) for p in range(lines // tall)], axis=0
        ).reshape(x_rows, depth, lanes)
        for r in range(x_rows + 2 * half):
            total = acc[r]
            for k in range(taps):
                if 0 <= r - k < x_rows:
                    total = total + px[v, k] * corrected[r - k]
            acc[r] = total

    sum_out[0] = acc[0:half].reshape(edge, lanes).astype(BF16)
    sum_out[1] = acc[half + x_rows :].reshape(edge, lanes).astype(BF16)
    sums = (sum_out, sum_in, sum_send_sem, sum_recv_sem)

    @pl.when(me > 0)
    def _():
        to_prev(*sums).start()

    @pl.when(me < n - 1)
    def _():
        to_next(*sums).start()

    pltpu.make_async_copy(send.at[0, relayed], send.at[0, relayed], line_send_sem.at[0]).wait()

    @pl.loop(1, views)
    def _(v):
        pltpu.make_async_copy(send.at[v, arrived], send.at[v, arrived], line_send_sem.at[v]).wait()

    @pl.when(me > 0)
    def _():
        to_prev(*sums).wait_send()
        pltpu.make_async_copy(sum_in.at[0], sum_in.at[0], sum_recv_sem.at[0]).wait()
        acc[half : 2 * half] = acc[half : 2 * half] + sum_in[0].astype(F32).reshape(half, depth, lanes)

    @pl.when(me < n - 1)
    def _():
        to_next(*sums).wait_send()
        pltpu.make_async_copy(sum_in.at[1], sum_in.at[1], sum_recv_sem.at[1]).wait()
        acc[x_rows : x_rows + half] = acc[x_rows : x_rows + half] + sum_in[1].astype(F32).reshape(half, depth, lanes)

    for x in range(x_rows):
        updated = est[x] * acc[half + x] * (1.0 / views)
        out[x] = jnp.where(jnp.full((depth, lanes), tissue[x]) == 1, updated, est[x])


def body(estimate, observed, interp, source_rows, tissue, psf_x, psf_y, psf_z):
    n = lax.axis_size("tile")
    x_rows, depth, lanes = estimate.shape
    views = observed.shape[0]
    lines = x_rows * depth
    cap = 2 * lines // n
    slots = n * cap
    taps = psf_x.shape[1]
    half = taps // 2
    if cap % 16 or lanes % cap or n * views != lanes or n % 2 or views * cap % lanes:
        return body_by_collectives(estimate, observed, interp, source_rows, tissue, psf_x, psf_y, psf_z)
    vmem = pl.BlockSpec(memory_space=pltpu.VMEM)
    edge = (2, half * depth, lanes)
    dma = pltpu.SemaphoreType.DMA
    return pl.pallas_call(
        functools.partial(sweep_kernel, n),
        out_shape=jax.ShapeDtypeStruct(estimate.shape, F32),
        in_specs=[pl.BlockSpec(memory_space=pl.ANY)] * 8,
        out_specs=vmem,
        scratch_shapes=[
            pltpu.VMEM(estimate.shape, F32),
            pltpu.VMEM(observed.shape, BF16),
            pltpu.VMEM(interp.shape, BF16),
            pltpu.VMEM(source_rows.shape, jnp.int32),
            pltpu.SMEM(tissue.shape, jnp.int32),
            pltpu.SMEM(psf_x.shape, F32),
            pltpu.SMEM(psf_y.shape, F32),
            pltpu.SMEM(psf_z.shape, F32),
            dma((8,)),
            pltpu.VMEM((x_rows + 2 * half, depth, lanes), F32),
            pltpu.VMEM(edge, BF16),
            pltpu.VMEM(edge, BF16),
            pltpu.VMEM((n, views * cap // lanes, lanes), F32),
            pltpu.VMEM((n, views * cap // lanes, lanes), F32),
            pltpu.VMEM((lanes, lanes), F32),
            pltpu.VMEM((n // 2, views * cap // lanes, lanes), F32),
            pltpu.VMEM((lanes, lanes), F32),
            pltpu.VMEM((x_rows, depth, lanes), BF16),
            pltpu.VMEM((n // 2 * cap, lanes), BF16),
            pltpu.VMEM((lines, lanes), F32),
            pltpu.VMEM((views, lines, slots), BF16),
            pltpu.VMEM((views, slots, lanes), BF16),
            pltpu.VMEM((views, slots, lanes), BF16),
            pltpu.VMEM((views, lines, lanes), F32),
            pltpu.VMEM((views, 2, lanes, lanes), BF16),
            pltpu.VMEM((views, 2, lanes, lanes), BF16),
            pltpu.VMEM((x_rows + 2 * half, depth, lanes), F32),
            pltpu.VMEM(edge, BF16),
            pltpu.VMEM(edge, BF16),
            dma((2,)), dma((2,)), dma, dma, dma((views,)), dma((views,)), dma((2,)), dma((2,)), dma, dma, dma, dma,
        ],
        compiler_params=pltpu.CompilerParams(
            collective_id=0, has_side_effects=True, vmem_limit_bytes=60 * 1024 * 1024
        ),
    )(estimate, observed, interp, source_rows, tissue, psf_x, psf_y, psf_z)


def solution(mesh):
    return jax.shard_map(
        body,
        mesh=mesh,
        in_specs=(
            P(("slab", "tile"), None, None),
            P(None, ("slab", "tile"), None, None),
            P(None, ("slab", "tile"), None, None),
            P(None, ("slab", "tile"), None),
            P(("slab", "tile")),
            P(),
            P(),
            P(),
        ),
        out_specs=P(("slab", "tile"), None, None),
        check_vma=False,
    )
```

```python
import functools

import jax
import jax.numpy as jnp
from jax import lax
from jax.experimental import pallas as pl
from jax.experimental.pallas import tpu as pltpu
from jax.sharding import PartitionSpec as P


def extended_2(value, sides, width):
    for axis, dim in sides:
        size, length = (lax.axis_size(axis), value.shape[dim])
        up = [(i, (i + 1) % size) for i in range(size - 1)]
        down = [(j, i) for i, j in up]
        last = lax.slice_in_dim(value, length - width, length, axis=dim)
        first = lax.slice_in_dim(value, 0, width, axis=dim)
        before = lax.ppermute(last, axis, up)
        after = lax.ppermute(first, axis, down)
        value = jnp.concatenate([before, value, after], axis=dim)
    return value


def taps_matrix(coeffs, count):
    half_taps = coeffs.shape[0] // 2
    offsets = jnp.arange(count)[:, None] - jnp.arange(count)[None, :] + half_taps
    inside = (offsets >= 0) & (offsets < coeffs.shape[0])
    return jnp.where(inside, coeffs[jnp.clip(offsets, 0, coeffs.shape[0] - 1)], jnp.float32(0.0))


def forward_x(extended, coeffs, out_rows):
    result = coeffs[0] * extended[0:out_rows]
    for offset in range(1, coeffs.shape[0]):
        result = result + coeffs[offset] * extended[offset : offset + out_rows]
    return result


def adjoint_x(extended, coeffs, out_rows):
    half_taps = coeffs.shape[0] // 2
    result = jnp.zeros((out_rows,) + extended.shape[1:], jnp.float32)
    for offset in range(coeffs.shape[0]):
        start = 2 * half_taps - offset
        result = result + coeffs[offset] * extended[start : start + out_rows]
    return result


def forward_yz(volume, matrix_z, matrix_y):
    volume = jnp.einsum("xzy,zw->xwy", volume, matrix_z, precision=lax.Precision.HIGHEST)
    return jnp.einsum("xzy,yu->xzu", volume, matrix_y, precision=lax.Precision.HIGHEST)


def adjoint_yz(volume, matrix_z, matrix_y):
    volume = jnp.einsum("xzu,yu->xzy", volume, matrix_y, precision=lax.Precision.HIGHEST)
    return jnp.einsum("xwy,zw->xzy", volume, matrix_z, precision=lax.Precision.HIGHEST)


def body_by_collectives(estimate, observed, interp, source_rows, tissue, psf_x, psf_y, psf_z):
    tile_rows, depth_cells, lane_cells = estimate.shape
    view_count = observed.shape[0]
    tile_count = lax.axis_size("tile")
    line_count = tile_rows * depth_cells
    capacity = 2 * line_count // tile_count
    half_taps = psf_x.shape[1] // 2
    flat_obs = observed.reshape(view_count * line_count, lane_cells)
    owners = (source_rows // tile_rows).reshape(view_count, line_count)
    payload = (
        jnp.arange(view_count, dtype=jnp.int32)[:, None, None] * line_count
        + source_rows % tile_rows * depth_cells
        + jnp.arange(depth_cells, dtype=jnp.int32)[None, None, :]
    ).reshape(view_count, line_count)
    owner_hits = (
        owners[:, :, None] == jnp.arange(tile_count, dtype=jnp.int32)[None, None, :]
    ).astype(jnp.int32)
    slot_index = jnp.sum((jnp.cumsum(owner_hits, axis=1) - 1) * owner_hits, axis=2)
    view_column = jnp.broadcast_to(
        jnp.arange(view_count, dtype=jnp.int32)[:, None], (view_count, line_count)
    )
    requests = jnp.zeros((tile_count, view_count, capacity), jnp.int32)
    requests = requests.at[owners, view_column, slot_index].set(payload)
    returned = lax.all_to_all(
        flat_obs[lax.all_to_all(requests, "tile", split_axis=0, concat_axis=0, tiled=True)],
        "tile",
        split_axis=0,
        concat_axis=0,
        tiled=True,
    )
    gathered_lines = returned[owners, view_column, slot_index]
    extended = extended_2(estimate.astype(jnp.bfloat16), (("tile", 0),), half_taps).astype(
        estimate.dtype
    )
    running = jnp.zeros_like(estimate)
    for view in range(view_count):
        taps_x = psf_x[view] / jnp.sum(psf_x[view])
        taps_y = psf_y[view] / jnp.sum(psf_y[view])
        taps_z = psf_z[view] / jnp.sum(psf_z[view])
        matrix_z = taps_matrix(taps_z, depth_cells)
        matrix_y = taps_matrix(taps_y, lane_cells)
        view_lines = gathered_lines[view]
        source_line = view_lines.reshape(tile_rows, depth_cells, lane_cells).astype(jnp.float32)
        next_line = jnp.concatenate([source_line[..., 1:], source_line[..., -1:]], axis=2)
        weight = interp[view].astype(jnp.float32)
        joined_view = weight * source_line + (1.0 - weight) * next_line
        blurred = forward_yz(forward_x(extended, taps_x, tile_rows), matrix_z, matrix_y)
        quotient = joined_view / blurred
        corrected = adjoint_yz(quotient, matrix_z, matrix_y)
        corrected_band = extended_2(
            corrected.astype(jnp.bfloat16), (("tile", 0),), half_taps
        ).astype(corrected.dtype)
        running = running + adjoint_x(corrected_band, taps_x, tile_rows)
    updated = estimate * running / view_count
    return jnp.where(tissue[:, None, None] == 1, updated, estimate)


MESH = pl.DeviceIdType.MESH
RELAY_AFTER = 3
F32 = jnp.float32
BF16 = jnp.bfloat16


def split(value):
    high = value.astype(BF16)
    return high, (value - high.astype(F32)).astype(BF16)


def dot(left, right):
    return jnp.dot(left, right, preferred_element_type=F32)


def dot_split(left, right):
    return dot(left[0], right[0]) + dot(left[0], right[1]) + dot(left[1], right[0])


def one_hot(mask):
    return jnp.where(mask, 1.0, 0.0).astype(BF16)


def sweep_kernel(
    n, est_far, obs_far, interp_far, rows_far, tissue_far, px_far, py_far, pz_far, out,
    est, obs, interp, rows, tissue, px, py, pz, in_sem,
    ext, halo_out, halo_in, req_out, req_in, req_t, relay_in, relay_t, raw, raw_send, slot_t, unpack, send, recv,
    inverse, adj_z, adj_y, acc, sum_out, sum_in,
    halo_send_sem, halo_recv_sem, req_send_sem, req_recv_sem, line_send_sem, line_recv_sem,
    sum_send_sem, sum_recv_sem, relay_send_sem, relay_recv_sem, raw_send_sem, raw_recv_sem,
):
    x_rows, depth, lanes = est.shape
    views = obs.shape[0]
    lines = x_rows * depth
    cap = 2 * lines // n
    slots = n * cap
    per_block = lanes // cap
    groups = views // per_block
    taps = px.shape[1]
    taps_z = pz.shape[1]
    half = taps // 2
    edge = half * depth
    me = lax.axis_index("tile")
    side = n // 2
    place = lax.rem(me, side)
    base = me - place
    partner = lax.rem(me + side, n)
    partner_base = partner - place

    barrier = pltpu.get_barrier_semaphore()
    pairs = (
        (rows_far, rows), (est_far, est), (obs_far, obs), (interp_far, interp), (px_far, px), (py_far, py), (pz_far, pz),
        (tissue_far, tissue),
    )
    loads = [pltpu.make_async_copy(far, near, in_sem.at[i]) for i, (far, near) in enumerate(pairs)]
    for load in loads:
        load.start()

    @pl.loop(1, n)
    def _(j):
        pl.semaphore_signal(barrier, inc=1, device_id={"tile": lax.rem(me + j, n)}, device_id_type=MESH)

    loads[0].wait()
    wanted = jnp.concatenate([rows[:, x, :] for x in range(x_rows)], axis=1)
    owner = wanted // x_rows
    line_id = lax.broadcasted_iota(jnp.int32, (views, lines), 1)
    payload = ((wanted - owner * x_rows) * depth + lax.rem(line_id, depth)).astype(F32)
    hits = [jnp.where(owner == o, 1.0, 0.0) for o in range(n)]
    earlier = one_hot(
        lax.broadcasted_iota(jnp.int32, (lines, lines), 0) < lax.broadcasted_iota(jnp.int32, (lines, lines), 1)
    )
    ranks = dot(jnp.concatenate(hits, axis=0).astype(BF16), earlier)
    rank = jnp.zeros((views, lines), F32)
    offset = jnp.zeros((views, lines), F32)
    for o in range(n):
        rank = rank + hits[o] * ranks[o * views : (o + 1) * views]
        offset = offset + hits[o] * float(o * cap)
    spot = rank + (lax.rem(lax.broadcasted_iota(jnp.int32, (views, lines), 0), per_block) * cap).astype(F32)
    empty = jnp.zeros((lanes - 2 * views, lines), F32)
    columns = jnp.concatenate([spot, rank + offset, empty], axis=0).T
    slot_t[...] = columns
    owner_id = lax.broadcasted_iota(jnp.int32, (n, lines), 0)
    lane_id = lax.broadcasted_iota(jnp.int32, (lines, lanes), 1).astype(F32)
    for g in range(groups):
        total = jnp.zeros((n, lanes), F32)
        for v in range(g * per_block, (g + 1) * per_block):
            theirs = jnp.where(owner[v : v + 1] == owner_id, payload[v : v + 1], 0.0).astype(BF16)
            total = total + dot(theirs, one_hot(columns[:, v : v + 1] == lane_id))
        req_out[:, g, :] = total

    loads[1].wait()
    halo_out[0] = est[0:half].reshape(edge, lanes).astype(BF16)
    halo_out[1] = est[x_rows - half : x_rows].reshape(edge, lanes).astype(BF16)
    loads[2].wait()
    pl.semaphore_wait(barrier, n - 1)

    def halo_copy(source, target, send_sem, recv_sem, side, device):
        return pltpu.make_async_remote_copy(
            src_ref=source.at[side], dst_ref=target.at[1 - side],
            send_sem=send_sem.at[side], recv_sem=recv_sem.at[1 - side],
            device_id={"tile": device}, device_id_type=MESH,
        )

    def to_prev(source, target, send_sem, recv_sem):
        return halo_copy(source, target, send_sem, recv_sem, 0, lax.rem(me + n - 1, n))

    def to_next(source, target, send_sem, recv_sem):
        return halo_copy(source, target, send_sem, recv_sem, 1, lax.rem(me + 1, n))

    def request_copy(j):
        d = lax.rem(me + j, n)
        return pltpu.make_async_remote_copy(
            src_ref=req_out.at[d], dst_ref=req_in.at[me],
            send_sem=req_send_sem, recv_sem=req_recv_sem,
            device_id={"tile": d}, device_id_type=MESH,
        )

    def relay_request_copy(j):
        d = base + lax.rem(place + j, side)
        return pltpu.make_async_remote_copy(
            src_ref=req_out.at[lax.rem(d + side, n)], dst_ref=relay_in.at[place],
            send_sem=relay_send_sem, recv_sem=relay_recv_sem,
            device_id={"tile": d}, device_id_type=MESH,
        )

    raw_copy = pltpu.make_async_remote_copy(
        src_ref=obs.at[0], dst_ref=raw, send_sem=raw_send_sem, recv_sem=raw_recv_sem,
        device_id={"tile": partner}, device_id_type=MESH,
    )

    @pl.loop(1, n)
    def _(j):
        request_copy(j).start()

    @pl.loop(1, side)
    def _(j):
        relay_request_copy(j).start()

    raw_copy.start()

    halos = (halo_out, halo_in, halo_send_sem, halo_recv_sem)

    @pl.when(me > 0)
    def _():
        to_prev(*halos).start()

    @pl.when(me < n - 1)
    def _():
        to_next(*halos).start()

    def turned_requests(ref, count):
        parts = [ref[:, g, :] for g in range(groups)]
        return jnp.concatenate(parts + [jnp.zeros((lanes - groups * count, lanes), F32)], axis=0).T

    req_in[me] = req_out[me]
    ahead = pl.ds(0, n - 1)
    pltpu.make_async_copy(req_in.at[ahead], req_in.at[ahead], req_recv_sem).wait()
    pltpu.make_async_copy(req_in.at[ahead], req_in.at[ahead], req_send_sem).wait()

    req_t[...] = turned_requests(req_in, n)
    line_lane = lax.broadcasted_iota(jnp.int32, (cap, lines), 1).astype(F32)
    own = pl.ds(pl.multiple_of(me * cap, cap), cap)

    def line_copy(v, source, target, d):
        return pltpu.make_async_remote_copy(
            src_ref=source, dst_ref=recv.at[v, target],
            send_sem=line_send_sem.at[v], recv_sem=line_recv_sem.at[v],
            device_id={"tile": d}, device_id_type=MESH,
        )

    def chunk(index):
        return pl.ds(pl.multiple_of(index * cap, cap), cap)

    def pack(v):
        group = v // per_block
        lines_of_view = req_t[pl.ds(pl.multiple_of((v - group * per_block) * cap, cap), cap), :]
        turned = pltpu.roll(lines_of_view, lax.rem(lanes - group * n, lanes), 1)
        chosen = jnp.concatenate([one_hot(turned[:, d : d + 1] == line_lane) for d in range(n)], axis=0)
        send[v] = dot(chosen, obs[v].reshape(lines, lanes)).astype(BF16)

    def send_view(v):
        pack(v)

        @pl.loop(0, side)
        def _(j):
            d = partner_base + lax.rem(place + j, side)
            line_copy(v, send.at[v, chunk(d)], own, d).start()

        @pl.loop(1, side)
        def _(j):
            d = base + lax.rem(place + j, side)
            line_copy(v, send.at[v, chunk(d)], own, d).start()

        recv[v, own] = send[v, own]

    pl.loop(1, RELAY_AFTER)(send_view)

    pltpu.make_async_copy(relay_in.at[pl.ds(0, side - 1)], relay_in.at[pl.ds(0, side - 1)], relay_recv_sem).wait()
    pltpu.make_async_copy(relay_in.at[pl.ds(0, side - 1)], relay_in.at[pl.ds(0, side - 1)], relay_send_sem).wait()
    relay_in[place] = req_out[partner]
    relay_t[...] = turned_requests(relay_in, side)
    others = relay_t[0:cap, :]
    chosen_raw = jnp.concatenate([one_hot(others[:, d : d + 1] == line_lane) for d in range(side)], axis=0)
    pack(0)
    raw_copy.wait()
    raw_send[...] = dot(chosen_raw, raw[...].reshape(lines, lanes)).astype(BF16)

    @pl.loop(1, side)
    def _(j):
        there = lax.rem(place + j, side)
        line_copy(0, raw_send.at[chunk(there)], chunk(partner), base + there).start()
        line_copy(0, send.at[0, chunk(base + there)], own, base + there).start()

    recv[0, own] = send[0, own]
    recv[0, chunk(partner)] = raw_send[chunk(place)]
    pl.loop(RELAY_AFTER, views)(send_view)

    ext[half : half + x_rows] = est[...]

    @pl.when(me > 0)
    def _():
        to_prev(*halos).wait_send()
        pltpu.make_async_copy(halo_in.at[0], halo_in.at[0], halo_recv_sem.at[0]).wait()
        ext[0:half] = halo_in[0].astype(F32).reshape(half, depth, lanes)

    @pl.when(me == 0)
    def _():
        ext[0:half] = jnp.zeros((half, depth, lanes), F32)

    @pl.when(me < n - 1)
    def _():
        to_next(*halos).wait_send()
        pltpu.make_async_copy(halo_in.at[1], halo_in.at[1], halo_recv_sem.at[1]).wait()
        ext[half + x_rows :] = halo_in[1].astype(F32).reshape(half, depth, lanes)

    @pl.when(me == n - 1)
    def _():
        ext[half + x_rows :] = jnp.zeros((half, depth, lanes), F32)

    for load in loads[3:]:
        load.wait()
    acc[...] = jnp.zeros(acc.shape, F32)
    copies = lanes // depth
    tall = copies * depth
    y_gap = lax.broadcasted_iota(jnp.int32, (lanes, lanes), 0) - lax.broadcasted_iota(jnp.int32, (lanes, lanes), 1)
    z_gap = (
        lax.rem(lax.broadcasted_iota(jnp.int32, (depth, tall), 1), depth)
        - lax.broadcasted_iota(jnp.int32, (depth, tall), 0)
    )
    same_block = (
        lax.broadcasted_iota(jnp.int32, (tall, tall), 0) // depth
        == lax.broadcasted_iota(jnp.int32, (tall, tall), 1) // depth
    )

    def total_of(ref, v, count):
        total = ref[v, 0]
        for k in range(1, count):
            total = total + ref[v, k]
        return total

    slot_lane = lax.broadcasted_iota(jnp.int32, (lines, slots), 1).astype(F32)

    @pl.loop(0, views)
    def _(v):
        unpack[v] = one_hot(pltpu.roll(slot_t[...], lax.rem(lanes - views - v, lanes), 1)[:, 0:1] == slot_lane)
        sum_x, sum_y, sum_z = total_of(px, v, taps), total_of(py, v, taps), total_of(pz, v, taps_z)
        scale_y = 1.0 / jnp.full((1, lanes), sum_y, F32)
        scale_z = 1.0 / jnp.full((1, tall), sum_z * sum_x, F32)
        fwd_y = jnp.zeros((lanes, lanes), F32)
        back_y = jnp.zeros((lanes, lanes), F32)
        for k in range(taps):
            fwd_y = jnp.where(y_gap == k - half, py[v, k], fwd_y)
            back_y = jnp.where(y_gap == half - k, py[v, k], back_y)
        fwd_z = jnp.zeros((depth, tall), F32)
        back_z = jnp.zeros((depth, tall), F32)
        for k in range(taps_z):
            fwd_z = jnp.where(z_gap == k - taps_z // 2, pz[v, k], fwd_z)
            back_z = jnp.where(z_gap == taps_z // 2 - k, pz[v, k], back_z)
        blocks_fwd = jnp.where(same_block, jnp.concatenate([fwd_z * scale_z] * copies, axis=0), 0.0)
        blocks_back = jnp.where(same_block, jnp.concatenate([back_z * scale_z] * copies, axis=0), 0.0)
        adj_z[v, 0], adj_z[v, 1] = split(blocks_back)
        adj_y[v, 0], adj_y[v, 1] = split(back_y * scale_y)
        z_parts = split(blocks_fwd)
        y_parts = split(fwd_y * scale_y)
        along_x = px[v, 0] * ext[0:x_rows]
        for k in range(1, taps):
            along_x = along_x + px[v, k] * ext[k : k + x_rows]
        along_x = along_x.reshape(lines, lanes)
        for part in range(lines // tall):
            piece = dot_split(z_parts, split(along_x[part * tall : (part + 1) * tall]))
            inverse[v, part * tall : (part + 1) * tall] = 1.0 / dot_split(split(piece), y_parts)

    last_lane = lax.broadcasted_iota(jnp.int32, (lines, lanes), 1) == lanes - 1
    arrived = pl.ds(0, slots - cap)

    sums = (sum_out, sum_in, sum_send_sem, sum_recv_sem)
    relayed = pl.ds(0, 2 * (side - 1) * cap)

    @pl.loop(0, views)
    def _(turn):
        v = jnp.where(turn < RELAY_AFTER - 1, turn + 1, jnp.where(turn == RELAY_AFTER - 1, 0, turn))

        @pl.when(v == 0)
        def _():
            pltpu.make_async_copy(recv.at[0, relayed], recv.at[0, relayed], line_recv_sem.at[0]).wait()

        @pl.when(v > 0)
        def _():
            pltpu.make_async_copy(recv.at[v, arrived], recv.at[v, arrived], line_recv_sem.at[v]).wait()

        line = dot(unpack[v], recv[v])
        following = jnp.where(last_lane, line, pltpu.roll(line, lanes - 1, 1))
        weight = interp[v].reshape(lines, lanes).astype(F32)
        quotient = (weight * line + (1.0 - weight) * following) * inverse[v]
        along_y = dot_split(split(quotient), (adj_y[v, 0], adj_y[v, 1]))
        z_parts = (adj_z[v, 0], adj_z[v, 1])
        corrected = jnp.concatenate(
            [dot_split(z_parts, split(along_y[p * tall : (p + 1) * tall])) for p in range(lines // tall)], axis=0
        ).reshape(x_rows, depth, lanes)

        def add_row(r):
            total = acc[r]
            for k in range(taps):
                if 0 <= r - k < x_rows:
                    total = total + px[v, k] * corrected[r - k]
            acc[r] = total

        for r in [*range(half), *range(half + x_rows, x_rows + 2 * half)]:
            add_row(r)

        @pl.when(turn == views - 1)
        def _():
            sum_out[0] = acc[0:half].reshape(edge, lanes).astype(BF16)
            sum_out[1] = acc[half + x_rows :].reshape(edge, lanes).astype(BF16)

            @pl.when(me > 0)
            def _():
                to_prev(*sums).start()

            @pl.when(me < n - 1)
            def _():
                to_next(*sums).start()

        for r in range(half, half + x_rows):
            add_row(r)


    pltpu.make_async_copy(send.at[0, relayed], send.at[0, relayed], line_send_sem.at[0]).wait()

    @pl.loop(1, views)
    def _(v):
        pltpu.make_async_copy(send.at[v, arrived], send.at[v, arrived], line_send_sem.at[v]).wait()

    @pl.when(me > 0)
    def _():
        to_prev(*sums).wait_send()
        pltpu.make_async_copy(sum_in.at[0], sum_in.at[0], sum_recv_sem.at[0]).wait()
        acc[half : 2 * half] = acc[half : 2 * half] + sum_in[0].astype(F32).reshape(half, depth, lanes)

    @pl.when(me < n - 1)
    def _():
        to_next(*sums).wait_send()
        pltpu.make_async_copy(sum_in.at[1], sum_in.at[1], sum_recv_sem.at[1]).wait()
        acc[x_rows : x_rows + half] = acc[x_rows : x_rows + half] + sum_in[1].astype(F32).reshape(half, depth, lanes)

    for x in range(x_rows):
        updated = est[x] * acc[half + x] * (1.0 / views)
        out[x] = jnp.where(jnp.full((depth, lanes), tissue[x]) == 1, updated, est[x])


def body(estimate, observed, interp, source_rows, tissue, psf_x, psf_y, psf_z):
    n = lax.axis_size("tile")
    x_rows, depth, lanes = estimate.shape
    views = observed.shape[0]
    lines = x_rows * depth
    cap = 2 * lines // n
    slots = n * cap
    taps = psf_x.shape[1]
    half = taps // 2
    if cap % 16 or lanes % cap or n * views != lanes or n % 2 or views * cap % lanes:
        return body_by_collectives(estimate, observed, interp, source_rows, tissue, psf_x, psf_y, psf_z)
    vmem = pl.BlockSpec(memory_space=pltpu.VMEM)
    edge = (2, half * depth, lanes)
    dma = pltpu.SemaphoreType.DMA
    return pl.pallas_call(
        functools.partial(sweep_kernel, n),
        out_shape=jax.ShapeDtypeStruct(estimate.shape, F32),
        in_specs=[pl.BlockSpec(memory_space=pl.ANY)] * 8,
        out_specs=vmem,
        scratch_shapes=[
            pltpu.VMEM(estimate.shape, F32),
            pltpu.VMEM(observed.shape, BF16),
            pltpu.VMEM(interp.shape, BF16),
            pltpu.VMEM(source_rows.shape, jnp.int32),
            pltpu.SMEM(tissue.shape, jnp.int32),
            pltpu.SMEM(psf_x.shape, F32),
            pltpu.SMEM(psf_y.shape, F32),
            pltpu.SMEM(psf_z.shape, F32),
            dma((8,)),
            pltpu.VMEM((x_rows + 2 * half, depth, lanes), F32),
            pltpu.VMEM(edge, BF16),
            pltpu.VMEM(edge, BF16),
            pltpu.VMEM((n, views * cap // lanes, lanes), F32),
            pltpu.VMEM((n, views * cap // lanes, lanes), F32),
            pltpu.VMEM((lanes, lanes), F32),
            pltpu.VMEM((n // 2, views * cap // lanes, lanes), F32),
            pltpu.VMEM((lanes, lanes), F32),
            pltpu.VMEM((x_rows, depth, lanes), BF16),
            pltpu.VMEM((n // 2 * cap, lanes), BF16),
            pltpu.VMEM((lines, lanes), F32),
            pltpu.VMEM((views, lines, slots), BF16),
            pltpu.VMEM((views, slots, lanes), BF16),
            pltpu.VMEM((views, slots, lanes), BF16),
            pltpu.VMEM((views, lines, lanes), F32),
            pltpu.VMEM((views, 2, lanes, lanes), BF16),
            pltpu.VMEM((views, 2, lanes, lanes), BF16),
            pltpu.VMEM((x_rows + 2 * half, depth, lanes), F32),
            pltpu.VMEM(edge, BF16),
            pltpu.VMEM(edge, BF16),
            dma((2,)), dma((2,)), dma, dma, dma((views,)), dma((views,)), dma((2,)), dma((2,)), dma, dma, dma, dma,
        ],
        compiler_params=pltpu.CompilerParams(
            collective_id=0, has_side_effects=True, vmem_limit_bytes=60 * 1024 * 1024
        ),
    )(estimate, observed, interp, source_rows, tissue, psf_x, psf_y, psf_z)


def solution(mesh):
    return jax.shard_map(
        body,
        mesh=mesh,
        in_specs=(
            P(("slab", "tile"), None, None),
            P(None, ("slab", "tile"), None, None),
            P(None, ("slab", "tile"), None, None),
            P(None, ("slab", "tile"), None),
            P(("slab", "tile")),
            P(),
            P(),
            P(),
        ),
        out_specs=P(("slab", "tile"), None, None),
        check_vma=False,
    )
```
